1024 devices in a mesh: dp: 64 (over z, core), expert: 16 (over y, x).
Axes of the slice: x: 4, y: 4, z: 32, core: 2. Of those that a mesh axis runs over, the one named last changes fastest.
Arguments:
- latents: bfloat16 [131072, 512], P(('dp', 'expert')), may hold values from -6 to 6
- routes: int32 [131072, 3], P(('dp', 'expert')), may hold values from 0 to 15, all different within a row; in each aligned block of 128 rows (0 to 127, 128 to 255, ...) at most 32 rows name the same one
- gate_level: int32 [131072, 3], P(('dp', 'expert')), may hold values from 1 to 256
- cotangent: bfloat16 [131072, 512], P(('dp', 'expert')), may hold values from -6 to 6
- w_gate: bfloat16 [16, 512, 1024], P('expert'), may hold values from -0.25 to 0.25
- w_up: bfloat16 [16, 512, 1024], P('expert'), may hold values from -0.25 to 0.25
- w_down: bfloat16 [16, 1024, 512], P('expert'), may hold values from -0.1875 to 0.1875
Outputs:
- latent_out: bfloat16 [131072, 512], P(('dp', 'expert'))
- grad_latents: bfloat16 [131072, 512], P(('dp', 'expert'))
- grad_down: float32 [16, 1024, 512], P('expert', 'dp')
The draws below stay inside these ranges and needn't reach their ends.
Inputs may be any that keep to these rules, and one draw needn't show every extreme that they name: `routes`: each row names 3 different experts; in the rows of one device no expert is named by more than 32 rows, and in every draw some expert is named by exactly 32 rows of some device.
All inputs are finite; a program needn't handle non-finite values.
Results may differ from the reference program's by a relative error of at most 0.0064.
Values may be sent and summed in bfloat16 or wider, within the bound.
A program may use at most 32 MiB of HBM per device.

```python
import math
import jax
import jax.numpy as jnp
import numpy as np
from jax import lax

L = 512
HID = 1024
EXPERTS = 16
TOP = 3
TOK_DEV = 128
CAP = 32
TOKENS = 131072


def set_ends(entries, stream_key, low, top_value):
    extent = entries.shape
    index_at = [jax.random.randint(jax.random.fold_in(stream_key, axis), (), 0, extent[axis]) for axis in range(len(extent))]
    entries = entries.at[tuple(index_at)].set(low)
    longest = extent.index(max(extent))
    index_at[longest] = (index_at[longest] + 1) % extent[longest]
    return entries.at[tuple(index_at)].set(top_value)


def level_of(rng, shape, shards, least, largest):
    gain = 1.0
    for axis_at, parts in shards:
        steps = jax.random.uniform(jax.random.fold_in(jax.random.fold_in(rng, 6), axis_at), (parts,), jnp.float32, least / len(shards), largest / len(shards))
        gain = gain * jnp.repeat(jnp.exp(steps), shape[axis_at] // parts).reshape((-1,) + (1,) * (len(shape) - 1 - axis_at))
    return gain


def shared_out(own_key, own, number, rows, number_of, top, limit, lean):
    ranking = jax.random.permutation(own_key, number_of)
    heavy_load, ordinary = shares(number_of, rows * top, limit, lean, True), shares(number_of, rows * top, limit, lean, False)
    places = jnp.arange(number_of)

    def named(lengths, rotation):
        used = int((lengths > 0).sum())
        fixed = max(1, used // 4)
        moved = fixed + (places - fixed + rotation * (used - fixed)) % max(1, number_of - fixed)
        return jnp.zeros((number_of,), jnp.int32).at[ranking[jnp.where(places < fixed, places, moved)]].set(jnp.asarray(lengths, jnp.int32))

    lengths = jnp.where(number % 4 == 0, named(heavy_load, number // 4), named(ordinary, number - number // 4 - 1))
    mixed = jax.random.permutation(jax.random.fold_in(own, 3), number_of)
    source_of, taker = mixed[0:number_of // 2 * 2:2], mixed[1:number_of // 2 * 2:2]
    margin = jnp.minimum(lengths[source_of] - 1, limit - lengths[taker]) // 2
    margin = jnp.where((source_of == ranking[0]) | (taker == ranking[0]) | (lengths[taker] == 0), 0, jnp.maximum(margin, 0))
    moved = jax.random.randint(jax.random.fold_in(own, 4), (number_of // 2,), 0, 1 << 20) % (margin + 1)
    lengths = lengths.at[source_of].add(-moved).at[taker].add(moved)
    items = jnp.searchsorted(jnp.cumsum(lengths), jnp.arange(rows * top), side="right").astype(jnp.int32)
    listing = items.reshape(top, rows).T
    listing = listing[jax.random.permutation(jax.random.fold_in(own, 1), rows)]
    rotation = jax.random.randint(jax.random.fold_in(own, 2), (rows, 1), 0, top)
    return jnp.take_along_axis(listing, (jnp.arange(top)[None, :] + rotation) % top, axis=1)


def shares(number_of, total, reach, lean, full):
    weights = [(1 << 20) // math.isqrt(rank ** lean) + 1 for rank in range(1, number_of + 1)]
    largest = reach if full else min(reach, max(-(-total // number_of), total * weights[0] // sum(weights)))
    least = 1 if total - largest >= number_of - 1 else 0
    counts, spare = [largest] + [least] * (number_of - 1), total - largest - least * (number_of - 1)
    while spare > 0:
        candidates = [i for i in range(1, number_of) if counts[i] < largest] or [i for i in range(1, number_of) if counts[i] < reach]
        pool, budget = sum([weights[i] for i in candidates]), spare
        for i in candidates:
            extra = min(reach - counts[i], max(1, budget * weights[i] // pool), spare)
            counts[i] = counts[i] + extra
            spare = spare - extra
    return np.array(counts)


def noise(key, extent, deviation, limit, cuts=(), held_as=jnp.bfloat16):
    factor_of = level_of(key, extent, cuts, -0.22, 0.18) if cuts else 1.0
    drawn = jax.random.normal(key, extent, jnp.float32) * deviation * factor_of
    return jnp.minimum(jnp.maximum(drawn, -limit), limit).astype(held_as)


def setup_inputs(seed: int = 0) -> dict:
    streams_of = jax.random.split(jax.random.key(seed), 8)
    latents = noise(streams_of[0], (TOKENS, L), 1.0, 6.0, ((0, 1024),))
    routes_keys = jax.random.split(jax.random.fold_in(streams_of[1], 1), TOKENS // TOK_DEV)
    routes_turns = jax.random.permutation(jax.random.fold_in(streams_of[1], 3), TOKENS // TOK_DEV)
    routes = jax.vmap(lambda own, number: shared_out(jax.random.fold_in(streams_of[1], 2), own, number, TOK_DEV, EXPERTS, TOP, CAP, 1))(routes_keys, routes_turns).reshape((TOKENS, TOP))
    gate_level = set_ends(jax.random.randint(streams_of[2], (TOKENS, TOP), 1, 257), jax.random.fold_in(streams_of[2], 1), 1, 256).astype(jnp.int32)
    cotangent = noise(streams_of[3], (TOKENS, L), 1.0, 6.0, ((0, 1024),))
    w_gate = noise(streams_of[4], (EXPERTS, L, HID), L ** -0.5, 0.25, ((0, 16),))
    w_up = noise(streams_of[5], (EXPERTS, L, HID), L ** -0.5, 0.25, ((0, 16),))
    w_down = noise(streams_of[6], (EXPERTS, HID, L), HID ** -0.5, 0.1875, ((0, 16),))
    return dict(latents=latents, routes=routes, gate_level=gate_level, cotangent=cotangent, w_gate=w_gate, w_up=w_up, w_down=w_down)


def reference(latents, routes, gate_level, cotangent, w_gate, w_up, w_down):
    blocks = TOKENS // TOK_DEV
    flat_routes = routes.reshape(blocks, TOK_DEV * TOP)
    expert_ids = jnp.arange(EXPERTS, dtype=jnp.int32)
    one_hot = (flat_routes[:, :, None] == expert_ids[None, None, :]).astype(jnp.int32)
    before = jnp.cumsum(one_hot, axis=1) - one_hot
    slot_index = jnp.sum(before * one_hot, axis=2).reshape(TOKENS, TOP)
    block_base = (jnp.arange(TOKENS, dtype=jnp.int32) // TOK_DEV) * CAP
    row_index = (block_base[:, None] + slot_index).astype(jnp.int32)
    levels = gate_level.astype(jnp.float32)
    weight = levels / jnp.sum(levels, axis=1, keepdims=True)
    cot_wide = cotangent.astype(jnp.float32)
    scaled = [(weight[:, route_pos:route_pos + 1] * cot_wide).astype(jnp.bfloat16) for route_pos in range(TOP)]
    buffer_rows = blocks * CAP

    def expert_step(carried, inputs):
        out_sum, grad_sum = carried
        gate_weights, up_weights, down_weights, expert_id = inputs
        dispatched = jnp.zeros((buffer_rows, L), jnp.bfloat16)
        row_grad = jnp.zeros((buffer_rows, L), jnp.bfloat16)
        for route_pos in range(TOP):
            chosen = routes[:, route_pos] == expert_id
            target = jnp.where(chosen, row_index[:, route_pos], buffer_rows).astype(jnp.int32)
            dispatched = dispatched.at[target].set(latents, mode="drop")
            row_grad = row_grad.at[target].set(scaled[route_pos], mode="drop")
        gate_pre = jnp.dot(dispatched, gate_weights, preferred_element_type=jnp.float32)
        up_pre = jnp.dot(dispatched, up_weights, preferred_element_type=jnp.float32)
        sigmoid_gate = jax.nn.sigmoid(gate_pre)
        activated = gate_pre * sigmoid_gate
        hidden = (activated * up_pre).astype(jnp.bfloat16)
        expert_out = jnp.dot(hidden, down_weights, preferred_element_type=jnp.float32).astype(jnp.bfloat16)
        grad_weights = jnp.dot(hidden.T, row_grad, preferred_element_type=jnp.float32)
        hidden_grad = jnp.dot(row_grad, down_weights.T, preferred_element_type=jnp.float32)
        derivative = sigmoid_gate * (1.0 + gate_pre * (1.0 - sigmoid_gate))
        gate_grad = (hidden_grad * up_pre * derivative).astype(jnp.bfloat16)
        up_grad = (hidden_grad * activated).astype(jnp.bfloat16)
        row_input = (jnp.dot(gate_grad, gate_weights.T, preferred_element_type=jnp.float32)
                     + jnp.dot(up_grad, up_weights.T, preferred_element_type=jnp.float32)).astype(jnp.bfloat16)
        for route_pos in range(TOP):
            chosen = (routes[:, route_pos] == expert_id)[:, None]
            safe_index = jnp.minimum(row_index[:, route_pos], buffer_rows - 1).astype(jnp.int32)
            picked = jnp.take(expert_out, safe_index, axis=0).astype(jnp.float32)
            out_sum = out_sum + jnp.where(chosen, weight[:, route_pos:route_pos + 1] * picked, jnp.float32(0.0))
            picked_grad = jnp.take(row_input, safe_index, axis=0).astype(jnp.float32)
            grad_sum = grad_sum + jnp.where(chosen, picked_grad, jnp.float32(0.0))
        return (out_sum, grad_sum), grad_weights

    start = (jnp.zeros((TOKENS, L), jnp.float32), jnp.zeros((TOKENS, L), jnp.float32))
    (out_sum, grad_sum), grad_down = lax.scan(expert_step, start, (w_gate, w_up, w_down, expert_ids))
    return out_sum.astype(jnp.bfloat16), grad_sum.astype(jnp.bfloat16), grad_down
```

```python
import jax
import jax.numpy as jnp
from jax import lax
from jax.experimental import pallas as pl
from jax.experimental.pallas import tpu as pltpu
from jax.sharding import PartitionSpec as P

CAP = 32
SIDE = 4
F32 = jnp.float32
BF16 = jnp.bfloat16
MESH = pl.DeviceIdType.MESH


def ring_distance(step):
    return min(step, SIDE - step)


PLACES = sorted(
    [(dy, dx) for dy in range(SIDE) for dx in range(SIDE)],
    key=lambda o: (ring_distance(o[0]) + ring_distance(o[1]), o),
)
SLOTS = len(PLACES)
FAR_FIRST = list(range(SLOTS - 1, 0, -1))
GROUP = 8
GROUPS = SLOTS // GROUP
ROWS = GROUP * CAP

PARENT = {}
for _r in range(-16, 16):
    if _r % 3:
        PARENT[_r] = _r - 1 if _r % 3 == 1 else _r + 1
for _r in (-15, -12, -6, 6, 12, 15):
    PARENT[_r] = 9 if _r > 0 else -9
PARENT.update({3: 0, -3: 0, 9: 0, -9: 0})
CHILDREN = {}
for _r, _q in PARENT.items():
    CHILDREN.setdefault(_q, []).append(_r)
ORDER = [15, -15, 12, -12, 6, -6, 9, -9, 3, -3, 0]
FIRST = [r for q in ORDER for r in CHILDREN[q] if r % 3]
SECOND = [15, -15, 12, -12, 6, -6, 3, -3]
THIRD = [9, -9]
HOPS = FIRST + SECOND + THIRD
HOP_AT = {r: i for i, r in enumerate(HOPS)}
Z_NEAR = (1, -1, 3, -3, 6, -6)


def kernel(
    lat_hbm, routes_hbm, level_hbm, cot_hbm, wg_hbm, wu_hbm, wd_hbm,
    out_ref, grad_ref, down_ref,
    lat, routes, level, cot, wg, wu, wd,
    key, share, place, place_w,
    sx, rx, sg, rg, se, re, si, ri,
    hid, hid_t, act, rate,
    own, sc, rc, hop_s, hop_r,
    load_sem, x_sem, g_sem, e_sem, i_sem, c_sem, h_sem,
):
    dp, ex = lax.axis_index("dp"), lax.axis_index("expert")
    z_count = lax.axis_size("dp") // 2
    z, c = dp // 2, lax.rem(dp, 2)
    y, x = ex // SIDE, lax.rem(ex, SIDE)

    def at_place(place_index, sign):
        dy, dx = PLACES[place_index]
        return lax.rem(y + sign * dy + SIDE, SIDE) * SIDE + lax.rem(x + sign * dx + SIDE, SIDE)

    def at_z(shift):
        return (lax.rem(z + shift + z_count, z_count) * 2 + c, ex)

    barrier = pltpu.get_barrier_semaphore()
    greeted = [(dp, at_place(j, 1)) for j in range(1, SLOTS)]
    greeted += [at_z(d) for d in Z_NEAR] + [(z * 2 + 1 - c, ex)]
    for device in greeted:
        pl.semaphore_signal(barrier, inc=1, device_id=device, device_id_type=MESH)

    loads = [
        pltpu.make_async_copy(source, target, load_sem.at[i])
        for i, (source, target) in enumerate(
            ((routes_hbm, routes), (level_hbm, level), (lat_hbm, lat), (cot_hbm, cot),
             (wg_hbm, wg), (wu_hbm, wu), (wd_hbm, wd))
        )
    ]
    for load in loads:
        load.start()
    loads[0].wait()
    loads[1].wait()

    tokens = lat.shape[0]
    lane = lax.broadcasted_iota(jnp.int32, (tokens, tokens), 1)
    row = lax.broadcasted_iota(jnp.int32, (tokens, tokens), 0)
    expert = lax.broadcasted_iota(jnp.int32, (SLOTS, tokens), 0)
    named = routes[...]
    levels = level[...].astype(F32)
    weight = levels / (levels[0:1] + levels[1:2] + levels[2:3])
    chosen_t = jnp.zeros((SLOTS, tokens), F32)
    share_t = jnp.zeros((SLOTS, tokens), F32)
    for k in range(3):
        hit = named[k:k + 1] == expert
        chosen_t = jnp.where(hit, 1.0, chosen_t)
        share_t = jnp.where(hit, weight[k:k + 1], share_t)
    share[...] = share_t
    earlier = (row < lane).astype(F32).astype(BF16)
    before = jnp.dot(chosen_t.astype(BF16), earlier, preferred_element_type=F32)
    key[...] = jnp.where(chosen_t > 0.0, before, -1.0)
    slot_of = lax.broadcasted_iota(jnp.int32, (CAP, tokens), 0).astype(F32)
    for j in range(SLOTS):
        e = at_place(j, 1)
        taken = key[pl.ds(e, 1), :] == slot_of
        place[j] = jnp.where(taken, 1.0, 0.0).astype(BF16)
        place_w[j] = jnp.where(taken, share[pl.ds(e, 1), :], 0.0)

    whole = SLOTS * CAP
    width = lat.shape[1]
    loads[2].wait()
    picked = place[...].reshape(whole, tokens)
    sx[...] = jnp.dot(picked, lat[...], preferred_element_type=F32).astype(BF16).reshape(
        SLOTS, CAP, width)

    def send(source, target, sems, j, sign):
        copy = pltpu.make_async_remote_copy(
            source.at[j], target.at[j], sems.at[0, j], sems.at[1, j],
            device_id=(dp, at_place(j, sign)), device_id_type=MESH)
        copy.start()
        return copy

    pl.semaphore_wait(barrier, len(greeted))
    x_copies = {j: send(sx, rx, x_sem, j, 1) for j in FAR_FIRST}
    rx[0] = sx[0]
    loads[3].wait()
    row_weight = jnp.sum(place_w[...].reshape(whole, tokens), axis=1, keepdims=True)
    scaled = row_weight * jnp.dot(picked, cot[...], preferred_element_type=F32)
    sg[...] = scaled.astype(BF16).reshape(SLOTS, CAP, width)
    g_copies = {j: send(sg, rg, g_sem, j, 1) for j in FAR_FIRST}
    rg[0] = sg[0]

    spread_w = place_w[...].reshape(whole, tokens).T
    high = spread_w.astype(BF16)
    low = (spread_w - high.astype(F32)).astype(BF16)
    spread_one = place[...].astype(F32).reshape(whole, tokens).T.astype(BF16)

    for load in loads[4:]:
        load.wait()
    hidden_width = wg.shape[1]
    tile = 256
    e_copies, i_copies = {}, {}
    for g in range(GROUPS):
        members = range(g * GROUP, (g + 1) * GROUP)
        for j in members:
            if j:
                x_copies[j].wait_recv()
        rows_in = rx[g * GROUP:(g + 1) * GROUP].reshape(ROWS, width)
        span = slice(g * ROWS, (g + 1) * ROWS)
        for n in range(hidden_width // tile):
            cols = slice(n * tile, (n + 1) * tile)
            gate = jnp.dot(rows_in, wg[:, cols], preferred_element_type=F32)
            up = jnp.dot(rows_in, wu[:, cols], preferred_element_type=F32)
            sig = jax.nn.sigmoid(gate)
            activated = gate * sig
            hidden = activated * up
            act[span, cols] = activated
            rate[span, cols] = up * (sig * (1.0 + gate * (1.0 - sig)))
            hid[:, cols] = hidden.astype(BF16)
            turned = hidden.T.astype(BF16).reshape(tile // 32, 2, 16, ROWS)
            chunk = slice(n * (tile // 32), (n + 1) * (tile // 32))
            hid_t[0, chunk, :, span] = turned[:, 0]
            hid_t[1, chunk, :, span] = turned[:, 1]
        result = jnp.dot(hid[...], wd[...], preferred_element_type=F32)
        se[g * GROUP:(g + 1) * GROUP] = result.astype(BF16).reshape(GROUP, CAP, width)
        for j in reversed(members):
            if j:
                e_copies[j] = send(se, re, e_sem, j, -1)
    re[0] = se[0]

    for j in range(1, SLOTS):
        g_copies[j].wait_recv()
    grads = rg[...].reshape(whole, width)
    half = z_count // 2
    c_copies = []
    for i in range(2):
        part = slice(i * half, (i + 1) * half)
        lhs = hid_t[1 - c, part].reshape(half * 16, whole)
        term = jnp.dot(lhs, grads, preferred_element_type=F32)
        sc[part] = term.astype(BF16).reshape(half, 16, width)
        copy = pltpu.make_async_remote_copy(
            sc.at[part], rc.at[part], c_sem.at[0, i], c_sem.at[1, i],
            device_id=(z * 2 + 1 - c, ex), device_id_type=MESH)
        copy.start()
        c_copies.append(copy)
    for i in range(2):
        part = slice(i * half, (i + 1) * half)
        lhs = hid_t[c, part].reshape(half * 16, whole)
        own[part] = jnp.dot(lhs, grads, preferred_element_type=F32).reshape(half, 16, width)

    def backward(g):
        members = range(g * GROUP, (g + 1) * GROUP)
        span = slice(g * ROWS, (g + 1) * ROWS)
        row_grad = rg[g * GROUP:(g + 1) * GROUP].reshape(ROWS, width)
        total = jnp.zeros((ROWS, width), F32)
        turn = (((1,), (1,)), ((), ()))
        for n in range(hidden_width // tile):
            cols = slice(n * tile, (n + 1) * tile)
            back = lax.dot_general(row_grad, wd[cols, :], turn, preferred_element_type=F32)
            gate_grad = (back * rate[span, cols]).astype(BF16)
            up_grad = (back * act[span, cols]).astype(BF16)
            total += lax.dot_general(gate_grad, wg[:, cols], turn, preferred_element_type=F32)
            total += lax.dot_general(up_grad, wu[:, cols], turn, preferred_element_type=F32)
        si[g * GROUP:(g + 1) * GROUP] = total.astype(BF16).reshape(GROUP, CAP, width)
        for j in reversed(members):
            if j:
                i_copies[j] = send(si, ri, i_sem, j, -1)

    hops = {}

    def partial(r):
        d = lax.rem(z - r + z_count, z_count)
        value = own[d] + rc[d].astype(F32)
        for child in CHILDREN.get(r, ()):
            hops[child].wait_recv()
            value = value + hop_r[HOP_AT[child]].astype(F32)
        return value

    def hop(r):
        i = HOP_AT[r]
        hop_s[i] = partial(r).astype(BF16)
        copy = pltpu.make_async_remote_copy(
            hop_s.at[i], hop_r.at[i], h_sem.at[0, i], h_sem.at[1, i],
            device_id=at_z(PARENT[r] - r), device_id_type=MESH)
        copy.start()
        hops[r] = copy

    backward(0)
    for copy in c_copies:
        copy.wait_recv()
    for r in FIRST:
        hop(r)
    backward(1)
    ri[0] = si[0]
    for r in SECOND:
        hop(r)
    for j in range(1, SLOTS):
        e_copies[j].wait_recv()
    returned = re[...].reshape(whole, width)
    summed = jnp.dot(high, returned, preferred_element_type=F32)
    summed += jnp.dot(low, returned, preferred_element_type=F32)
    out_ref[...] = summed.astype(BF16)
    for r in THIRD:
        hop(r)
    for j in range(1, SLOTS):
        i_copies[j].wait_recv()
    grad_ref[...] = jnp.dot(
        spread_one, ri[...].reshape(whole, width), preferred_element_type=F32).astype(BF16)
    down_ref[...] = partial(0)

    for copies in (x_copies, g_copies, e_copies, i_copies, hops):
        for copy in copies.values():
            copy.wait_send()
    for copy in c_copies:
        copy.wait_send()


def local(latents, routes, gate_level, cotangent, w_gate, w_up, w_down):
    tokens, width = latents.shape
    hidden = w_gate.shape[2]
    whole = SLOTS * CAP
    z_count = lax.axis_size("dp") // 2
    block = (SLOTS, CAP, width)
    hop_count = len(HOPS)
    anywhere = pl.BlockSpec(memory_space=pl.ANY)
    in_vmem = pl.BlockSpec(memory_space=pltpu.VMEM)
    dma = pltpu.SemaphoreType.DMA
    latent_out, grad_latents, grad_down = pl.pallas_call(
        kernel,
        out_shape=(
            jax.ShapeDtypeStruct((tokens, width), BF16),
            jax.ShapeDtypeStruct((tokens, width), BF16),
            jax.ShapeDtypeStruct((16, width), F32),
        ),
        in_specs=[anywhere] * 7,
        out_specs=(in_vmem,) * 3,
        scratch_shapes=[
            pltpu.VMEM(latents.shape, BF16),
            pltpu.VMEM(routes.shape[::-1], jnp.int32),
            pltpu.VMEM(gate_level.shape[::-1], jnp.int32),
            pltpu.VMEM(cotangent.shape, BF16),
            pltpu.VMEM((width, hidden), BF16),
            pltpu.VMEM((width, hidden), BF16),
            pltpu.VMEM((hidden, width), BF16),
            pltpu.VMEM((SLOTS, tokens), F32),
            pltpu.VMEM((SLOTS, tokens), F32),
            pltpu.VMEM((SLOTS, CAP, tokens), BF16),
            pltpu.VMEM((SLOTS, CAP, tokens), F32),
        ] + [pltpu.VMEM(block, BF16)] * 8 + [
            pltpu.VMEM((ROWS, hidden), BF16),
            pltpu.VMEM((2, z_count, 16, whole), BF16),
            pltpu.VMEM((whole, hidden), F32),
            pltpu.VMEM((whole, hidden), F32),
            pltpu.VMEM((z_count, 16, width), F32),
            pltpu.VMEM((z_count, 16, width), BF16),
            pltpu.VMEM((z_count, 16, width), BF16),
            pltpu.VMEM((hop_count, 16, width), BF16),
            pltpu.VMEM((hop_count, 16, width), BF16),
            dma((7,)), dma((2, SLOTS)), dma((2, SLOTS)), dma((2, SLOTS)), dma((2, SLOTS)),
            dma((2, 2)), dma((2, hop_count)),
        ],
        compiler_params=pltpu.CompilerParams(
            collective_id=0, has_side_effects=True, vmem_limit_bytes=56 << 20),
        name="moe",
    )(latents, routes.T, gate_level.T, cotangent, w_gate[0], w_up[0], w_down[0])
    return latent_out, grad_latents, grad_down[None]


def solution(mesh):
    return jax.shard_map(
        local,
        mesh=mesh,
        in_specs=(
            P(("dp", "expert"), None),
            P(("dp", "expert"), None),
            P(("dp", "expert"), None),
            P(("dp", "expert"), None),
            P("expert", None, None),
            P("expert", None, None),
            P("expert", None, None),
        ),
        out_specs=(P(("dp", "expert"), None), P(("dp", "expert"), None), P("expert", "dp", None)),
        check_vma=False,
    )
```

```python
import jax
import jax.numpy as jnp
from jax import lax
from jax.experimental import pallas as pl
from jax.experimental.pallas import tpu as pltpu
from jax.sharding import PartitionSpec as P

CAP = 32
SIDE = 4
F32 = jnp.float32
BF16 = jnp.bfloat16
MESH = pl.DeviceIdType.MESH


def ring_distance(step):
    return min(step, SIDE - step)


PLACES = sorted(
    [(dy, dx) for dy in range(SIDE) for dx in range(SIDE)],
    key=lambda o: (ring_distance(o[0]) + ring_distance(o[1]), o),
)
SLOTS = len(PLACES)
GROUP = 8
GROUPS = SLOTS // GROUP
ROWS = GROUP * CAP

PARENT = {}
for _r, _q in {
    1: 0, 2: 1, 3: 2, 4: 0, 5: 4, 6: 5, 7: 9, 8: 9, 9: 10, 10: 0, 11: 10, 12: 10, 13: 14, 14: 10, 15: 14,
}.items():
    PARENT[_r], PARENT[-_r] = _q, -_q
PARENT[-16] = -14
CHILDREN = {}
for _r, _q in PARENT.items():
    CHILDREN.setdefault(_q, []).append(_r)
LEAVES = [-16, -15, -13, 13, 15, -7, 7, -8, 8, -6, 6, -12, 12, -11, 11, -3, 3]
INNER = [14, -14, 5, -5, 2, -2, -9, 9, 4, -4, 1, -1, -10, 10]
HOPS = LEAVES + INNER
HOP_AT = {r: i for i, r in enumerate(HOPS)}
RELAY = 4
Z_NEAR = (1, -1, 2, -2, 3, -3, RELAY, -RELAY)


def kernel(
    lat_hbm, routes_hbm, level_hbm, cot_hbm, wg_hbm, wu_hbm, wd_hbm,
    out_ref, grad_ref, down_ref,
    lat, routes, level, cot, wg, wu, wd,
    key, share, place, place_w,
    sx, rx, sg, rg, se, re, si, ri,
    hid, hid_t, act, rate,
    own, sc, rc, hop_s, hop_r,
    load_sem, x_sem, g_sem, e_sem, i_sem, c_sem, h_sem, relay_sem,
):
    dp, ex = lax.axis_index("dp"), lax.axis_index("expert")
    z_count = lax.axis_size("dp") // 2
    z, c = dp // 2, lax.rem(dp, 2)
    y, x = ex // SIDE, lax.rem(ex, SIDE)

    def at_place(place_index, sign):
        dy, dx = PLACES[place_index]
        return lax.rem(y + sign * dy + SIDE, SIDE) * SIDE + lax.rem(x + sign * dx + SIDE, SIDE)

    def at_z(shift):
        return (lax.rem(z + shift + z_count, z_count) * 2 + c, ex)

    loads = [
        pltpu.make_async_copy(source, target, load_sem.at[i])
        for i, (source, target) in enumerate(
            ((routes_hbm, routes), (level_hbm, level), (lat_hbm, lat), (cot_hbm, cot),
             (wg_hbm, wg), (wu_hbm, wu), (wd_hbm, wd))
        )
    ]
    for load in loads[:4]:
        load.start()

    barrier = pltpu.get_barrier_semaphore()
    greeted = [(dp, at_place(j, 1)) for j in range(1, SLOTS)]
    greeted += [at_z(d) for d in Z_NEAR] + [(z * 2 + 1 - c, ex)]
    for device in greeted:
        pl.semaphore_signal(barrier, inc=1, device_id=device, device_id_type=MESH)

    loads[0].wait()
    loads[1].wait()

    tokens = lat.shape[0]
    lane = lax.broadcasted_iota(jnp.int32, (tokens, tokens), 1)
    row = lax.broadcasted_iota(jnp.int32, (tokens, tokens), 0)
    expert = lax.broadcasted_iota(jnp.int32, (SLOTS, tokens), 0)
    named = routes[...]
    levels = level[...].astype(F32)
    weight = levels / (levels[0:1] + levels[1:2] + levels[2:3])
    chosen_t = jnp.zeros((SLOTS, tokens), F32)
    share_t = jnp.zeros((SLOTS, tokens), F32)
    for k in range(3):
        hit = named[k:k + 1] == expert
        chosen_t = jnp.where(hit, 1.0, chosen_t)
        share_t = jnp.where(hit, weight[k:k + 1], share_t)
    share[...] = share_t
    earlier = (row < lane).astype(F32).astype(BF16)
    before = jnp.dot(chosen_t.astype(BF16), earlier, preferred_element_type=F32)
    key[...] = jnp.where(chosen_t > 0.0, before, -1.0)
    slot_of = lax.broadcasted_iota(jnp.int32, (CAP, tokens), 0).astype(F32)
    for j in range(SLOTS):
        e = at_place(j, 1)
        taken = key[pl.ds(e, 1), :] == slot_of
        place[j] = jnp.where(taken, 1.0, 0.0).astype(BF16)
        place_w[j] = jnp.where(taken, share[pl.ds(e, 1), :], 0.0)

    whole = SLOTS * CAP
    width = lat.shape[1]
    parts = [slice(g * GROUP, (g + 1) * GROUP) for g in reversed(range(GROUPS))]

    def send(source, target, sems, j, sign):
        copy = pltpu.make_async_remote_copy(
            source.at[j], target.at[j], sems.at[0, j], sems.at[1, j],
            device_id=(dp, at_place(j, sign)), device_id_type=MESH)
        copy.start()
        return copy

    def send_part(copies, source, target, sems, part, sign):
        for j in reversed(range(part.start, part.stop)):
            if j:
                copies[j] = send(source, target, sems, j, sign)

    x_copies, g_copies, e_copies, i_copies = {}, {}, {}, {}
    loads[2].wait()
    loads[3].wait()
    for load in loads[4:]:
        load.start()
    for n, part in enumerate(parts):
        picked = place[part].reshape(ROWS, tokens)
        sx[part] = jnp.dot(picked, lat[...], preferred_element_type=F32).astype(BF16).reshape(
            GROUP, CAP, width)
        if n == 0:
            pl.semaphore_wait(barrier, len(greeted))
        send_part(x_copies, sx, rx, x_sem, part, 1)
    for part in parts:
        picked = place[part].reshape(ROWS, tokens)
        row_weight = jnp.sum(place_w[part].reshape(ROWS, tokens), axis=1, keepdims=True)
        scaled = row_weight * jnp.dot(picked, cot[...], preferred_element_type=F32)
        sg[part] = scaled.astype(BF16).reshape(GROUP, CAP, width)
        send_part(g_copies, sg, rg, g_sem, part, 1)
    for shift in (RELAY, -RELAY):
        pl.semaphore_signal(relay_sem, inc=1, device_id=at_z(shift), device_id_type=MESH)
    rx[0] = sx[0]
    rg[0] = sg[0]

    spread_w = place_w[...].reshape(whole, tokens).T
    high = spread_w.astype(BF16)
    low = (spread_w - high.astype(F32)).astype(BF16)
    spread_one = place[...].astype(F32).reshape(whole, tokens).T.astype(BF16)

    for load in loads[4:]:
        load.wait()
    hidden_width = wg.shape[1]
    tile = 256
    for g in reversed(range(GROUPS)):
        members = range(g * GROUP, (g + 1) * GROUP)
        for j in members:
            if j:
                x_copies[j].wait_recv()
        rows_in = rx[g * GROUP:(g + 1) * GROUP].reshape(ROWS, width)
        span = slice(g * ROWS, (g + 1) * ROWS)
        for n in range(hidden_width // tile):
            cols = slice(n * tile, (n + 1) * tile)
            gate = jnp.dot(rows_in, wg[:, cols], preferred_element_type=F32)
            up = jnp.dot(rows_in, wu[:, cols], preferred_element_type=F32)
            sig = jax.nn.sigmoid(gate)
            activated = gate * sig
            hidden = activated * up
            act[span, cols] = activated
            rate[span, cols] = up * (sig * (1.0 + gate * (1.0 - sig)))
            hid[:, cols] = hidden.astype(BF16)
            turned = hidden.T.astype(BF16).reshape(tile // 32, 2, 16, ROWS)
            chunk = slice(n * (tile // 32), (n + 1) * (tile // 32))
            hid_t[0, chunk, :, span] = turned[:, 0]
            hid_t[1, chunk, :, span] = turned[:, 1]
        result = jnp.dot(hid[...], wd[...], preferred_element_type=F32)
        se[g * GROUP:(g + 1) * GROUP] = result.astype(BF16).reshape(GROUP, CAP, width)
    re[0] = se[0]

    for j in range(1, SLOTS):
        g_copies[j].wait_recv()
    grads = rg[...].reshape(whole, width)
    half = z_count // 2
    c_copies = []
    for i in range(2):
        part = slice(i * half, (i + 1) * half)
        lhs = hid_t[1 - c, part].reshape(half * 16, whole)
        term = jnp.dot(lhs, grads, preferred_element_type=F32)
        sc[part] = term.astype(BF16).reshape(half, 16, width)
        copy = pltpu.make_async_remote_copy(
            sc.at[part], rc.at[part], c_sem.at[0, i], c_sem.at[1, i],
            device_id=(z * 2 + 1 - c, ex), device_id_type=MESH)
        copy.start()
        c_copies.append(copy)
    for part in parts:
        send_part(e_copies, se, re, e_sem, part, -1)
    for i in range(2):
        part = slice(i * half, (i + 1) * half)
        lhs = hid_t[c, part].reshape(half * 16, whole)
        own[part] = jnp.dot(lhs, grads, preferred_element_type=F32).reshape(half, 16, width)

    def backward(g):
        span = slice(g * ROWS, (g + 1) * ROWS)
        row_grad = rg[g * GROUP:(g + 1) * GROUP].reshape(ROWS, width)
        total = jnp.zeros((ROWS, width), F32)
        turn = (((1,), (1,)), ((), ()))
        for n in range(hidden_width // tile):
            cols = slice(n * tile, (n + 1) * tile)
            back = lax.dot_general(row_grad, wd[cols, :], turn, preferred_element_type=F32)
            gate_grad = (back * rate[span, cols]).astype(BF16)
            up_grad = (back * act[span, cols]).astype(BF16)
            total += lax.dot_general(gate_grad, wg[:, cols], turn, preferred_element_type=F32)
            total += lax.dot_general(up_grad, wu[:, cols], turn, preferred_element_type=F32)
        si[g * GROUP:(g + 1) * GROUP] = total.astype(BF16).reshape(GROUP, CAP, width)
        send_part(i_copies, si, ri, i_sem, slice(g * GROUP, (g + 1) * GROUP), -1)

    hops = {}

    def partial(r):
        d = lax.rem(z - r + z_count, z_count)
        value = own[d] + rc[d].astype(F32)
        for child in CHILDREN.get(r, ()):
            hops[child].wait_recv()
            value = value + hop_r[HOP_AT[child]].astype(F32)
        return value

    def hop(r):
        i = HOP_AT[r]
        hop_s[i] = partial(r).astype(BF16)
        copy = pltpu.make_async_remote_copy(
            hop_s.at[i], hop_r.at[i], h_sem.at[0, i], h_sem.at[1, i],
            device_id=at_z(PARENT[r] - r), device_id_type=MESH)
        copy.start()
        hops[r] = copy

    backward(1)
    pl.semaphore_wait(relay_sem, 2)
    for copy in c_copies:
        copy.wait_recv()
    for r in LEAVES:
        hop(r)
    backward(0)
    ri[0] = si[0]
    for r in INNER:
        hop(r)
    for j in range(1, SLOTS):
        e_copies[j].wait_recv()
    returned = re[...].reshape(whole, width)
    summed = jnp.dot(high, returned, preferred_element_type=F32)
    summed += jnp.dot(low, returned, preferred_element_type=F32)
    out_ref[...] = summed.astype(BF16)
    for j in range(1, SLOTS):
        i_copies[j].wait_recv()
    grad_ref[...] = jnp.dot(
        spread_one, ri[...].reshape(whole, width), preferred_element_type=F32).astype(BF16)
    down_ref[...] = partial(0)

    for copies in (x_copies, g_copies, e_copies, i_copies, hops):
        for copy in copies.values():
            copy.wait_send()
    for copy in c_copies:
        copy.wait_send()


def local(latents, routes, gate_level, cotangent, w_gate, w_up, w_down):
    tokens, width = latents.shape
    hidden = w_gate.shape[2]
    whole = SLOTS * CAP
    z_count = lax.axis_size("dp") // 2
    block = (SLOTS, CAP, width)
    hop_count = len(HOPS)
    anywhere = pl.BlockSpec(memory_space=pl.ANY)
    in_vmem = pl.BlockSpec(memory_space=pltpu.VMEM)
    dma = pltpu.SemaphoreType.DMA
    latent_out, grad_latents, grad_down = pl.pallas_call(
        kernel,
        out_shape=(
            pltpu.VMEM((tokens, width), BF16),
            pltpu.VMEM((tokens, width), BF16),
            pltpu.VMEM((16, width), F32),
        ),
        in_specs=[anywhere] * 7,
        out_specs=(in_vmem,) * 3,
        scratch_shapes=[
            pltpu.VMEM(latents.shape, BF16),
            pltpu.VMEM(routes.shape[::-1], jnp.int32),
            pltpu.VMEM(gate_level.shape[::-1], jnp.int32),
            pltpu.VMEM(cotangent.shape, BF16),
            pltpu.VMEM((width, hidden), BF16),
            pltpu.VMEM((width, hidden), BF16),
            pltpu.VMEM((hidden, width), BF16),
            pltpu.VMEM((SLOTS, tokens), F32),
            pltpu.VMEM((SLOTS, tokens), F32),
            pltpu.VMEM((SLOTS, CAP, tokens), BF16),
            pltpu.VMEM((SLOTS, CAP, tokens), F32),
        ] + [pltpu.VMEM(block, BF16)] * 8 + [
            pltpu.VMEM((ROWS, hidden), BF16),
            pltpu.VMEM((2, z_count, 16, whole), BF16),
            pltpu.VMEM((whole, hidden), F32),
            pltpu.VMEM((whole, hidden), F32),
            pltpu.VMEM((z_count, 16, width), F32),
            pltpu.VMEM((z_count, 16, width), BF16),
            pltpu.VMEM((z_count, 16, width), BF16),
            pltpu.VMEM((hop_count, 16, width), BF16),
            pltpu.VMEM((hop_count, 16, width), BF16),
            dma((7,)), dma((2, SLOTS)), dma((2, SLOTS)), dma((2, SLOTS)), dma((2, SLOTS)),
            dma((2, 2)), dma((2, hop_count)), pltpu.SemaphoreType.REGULAR,
        ],
        compiler_params=pltpu.CompilerParams(
            collective_id=0, has_side_effects=True, vmem_limit_bytes=56 << 20),
        name="moe",
    )(latents, routes.T, gate_level.T, cotangent, w_gate[0], w_up[0], w_down[0])
    return latent_out, grad_latents, grad_down[None]


def solution(mesh):
    return jax.shard_map(
        local,
        mesh=mesh,
        in_specs=(
            P(("dp", "expert"), None),
            P(("dp", "expert"), None),
            P(("dp", "expert"), None),
            P(("dp", "expert"), None),
            P("expert", None, None),
            P("expert", None, None),
            P("expert", None, None),
        ),
        out_specs=(P(("dp", "expert"), None), P(("dp", "expert"), None), P("expert", "dp", None)),
        check_vma=False,
    )
```

```python
import jax
import jax.numpy as jnp
from jax import lax
from jax.experimental import pallas as pl
from jax.experimental.pallas import tpu as pltpu
from jax.sharding import PartitionSpec as P

CAP = 32
SIDE = 4
F32 = jnp.float32
BF16 = jnp.bfloat16
MESH = pl.DeviceIdType.MESH


def ring_distance(step):
    return min(step, SIDE - step)


PLACES = sorted(
    [(dy, dx) for dy in range(SIDE) for dx in range(SIDE)],
    key=lambda o: (ring_distance(o[0]) + ring_distance(o[1]), o),
)
SLOTS = len(PLACES)
GROUP = 8
GROUPS = SLOTS // GROUP
ROWS = GROUP * CAP

PARENT = {}
for _r, _q in {
    1: 0, 2: 1, 3: 2, 4: 0, 5: 4, 6: 5, 7: 9, 8: 9, 9: 10, 10: 0, 11: 10, 12: 10, 13: 14, 14: 10, 15: 14,
}.items():
    PARENT[_r], PARENT[-_r] = _q, -_q
PARENT[-16] = -14
CHILDREN = {}
for _r, _q in PARENT.items():
    CHILDREN.setdefault(_q, []).append(_r)
LEAVES = [-16, -15, -13, 13, 15, -7, 7, -8, 8, -6, 6, -12, 12, -11, 11, -3, 3]
INNER = [14, -14, 5, -5, 2, -2, -9, 9, 4, -4, 1, -1, -10, 10]
HOPS = LEAVES + INNER
HOP_AT = {r: i for i, r in enumerate(HOPS)}
PIECES = 2
LATER = [(0, -14), (0, 14), (0, -9), (0, 9), (0, -5), (0, 5), (0, -2), (0, 2), (1, 14), (1, -14), (1, -9), (1, 5), (1, -5), (1, 9), (1, 2), (1, -2), (0, 4), (0, -4), (0, 1), (0, -1), (0, 10), (0, -10), (1, 4), (1, -4), (1, 10), (1, -10), (1, 1), (1, -1)]
RELAY = 4
Z_NEAR = (1, -1, 2, -2, 3, -3, RELAY, -RELAY)


def kernel(
    lat_hbm, routes_hbm, level_hbm, cot_hbm, wg_hbm, wu_hbm, wd_hbm,
    out_ref, grad_ref, down_ref,
    lat, routes, level, cot, wg, wu, wd,
    key, share, place, place_w,
    sx, rx, sg, rg, se, re, si, ri,
    hid, hid_t, act, rate,
    own, sc, rc, hop_s, hop_r,
    load_sem, x_sem, g_sem, e_sem, i_sem, c_sem, h_sem, relay_sem,
):
    dp, ex = lax.axis_index("dp"), lax.axis_index("expert")
    z_count = lax.axis_size("dp") // 2
    z, c = dp // 2, lax.rem(dp, 2)
    y, x = ex // SIDE, lax.rem(ex, SIDE)

    def at_place(place_index, sign):
        dy, dx = PLACES[place_index]
        return lax.rem(y + sign * dy + SIDE, SIDE) * SIDE + lax.rem(x + sign * dx + SIDE, SIDE)

    def at_z(shift):
        return (lax.rem(z + shift + z_count, z_count) * 2 + c, ex)

    loads = [
        pltpu.make_async_copy(source, target, load_sem.at[i])
        for i, (source, target) in enumerate(
            ((routes_hbm, routes), (level_hbm, level), (lat_hbm, lat), (cot_hbm, cot),
             (wg_hbm, wg), (wu_hbm, wu), (wd_hbm, wd))
        )
    ]
    for load in loads[:4]:
        load.start()

    barrier = pltpu.get_barrier_semaphore()
    greeted = [(dp, at_place(j, 1)) for j in range(1, SLOTS)]
    greeted += [at_z(d) for d in Z_NEAR] + [(z * 2 + 1 - c, ex)]
    for device in greeted:
        pl.semaphore_signal(barrier, inc=1, device_id=device, device_id_type=MESH)

    loads[0].wait()
    loads[1].wait()

    tokens = lat.shape[0]
    lane = lax.broadcasted_iota(jnp.int32, (tokens, tokens), 1)
    row = lax.broadcasted_iota(jnp.int32, (tokens, tokens), 0)
    expert = lax.broadcasted_iota(jnp.int32, (SLOTS, tokens), 0)
    named = routes[...]
    levels = level[...].astype(F32)
    weight = levels / (levels[0:1] + levels[1:2] + levels[2:3])
    chosen_t = jnp.zeros((SLOTS, tokens), F32)
    share_t = jnp.zeros((SLOTS, tokens), F32)
    for k in range(3):
        hit = named[k:k + 1] == expert
        chosen_t = jnp.where(hit, 1.0, chosen_t)
        share_t = jnp.where(hit, weight[k:k + 1], share_t)
    share[...] = share_t
    earlier = (row < lane).astype(F32).astype(BF16)
    before = jnp.dot(chosen_t.astype(BF16), earlier, preferred_element_type=F32)
    key[...] = jnp.where(chosen_t > 0.0, before, -1.0)
    slot_of = lax.broadcasted_iota(jnp.int32, (CAP, tokens), 0).astype(F32)
    for j in range(SLOTS):
        e = at_place(j, 1)
        taken = key[pl.ds(e, 1), :] == slot_of
        place[j] = jnp.where(taken, 1.0, 0.0).astype(BF16)
        place_w[j] = jnp.where(taken, share[pl.ds(e, 1), :], 0.0)

    whole = SLOTS * CAP
    width = lat.shape[1]
    parts = [slice(g * GROUP, (g + 1) * GROUP) for g in reversed(range(GROUPS))]

    def send(source, target, sems, j, sign):
        copy = pltpu.make_async_remote_copy(
            source.at[j], target.at[j], sems.at[0, j], sems.at[1, j],
            device_id=(dp, at_place(j, sign)), device_id_type=MESH)
        copy.start()
        return copy

    def send_part(copies, source, target, sems, part, sign):
        for j in reversed(range(part.start, part.stop)):
            if j:
                copies[j] = send(source, target, sems, j, sign)

    x_copies, e_copies, i_copies = {}, {}, {}
    g_copies = [{} for _ in range(PIECES)]
    piece = width // PIECES
    loads[2].wait()
    loads[3].wait()
    for load in loads[4:]:
        load.start()
    for n, part in enumerate(parts):
        picked = place[part].reshape(ROWS, tokens)
        sx[part] = jnp.dot(picked, lat[...], preferred_element_type=F32).astype(BF16).reshape(
            GROUP, CAP, width)
        if n == 0:
            pl.semaphore_wait(barrier, len(greeted))
        send_part(x_copies, sx, rx, x_sem, part, 1)
    for part in parts:
        picked = place[part].reshape(ROWS, tokens)
        row_weight = jnp.sum(place_w[part].reshape(ROWS, tokens), axis=1, keepdims=True)
        scaled = row_weight * jnp.dot(picked, cot[...], preferred_element_type=F32)
        scaled = scaled.astype(BF16)
        for p in range(PIECES):
            sg[p, part] = scaled[:, p * piece:(p + 1) * piece].reshape(GROUP, CAP, piece)
        send_part(g_copies[0], sg.at[0], rg.at[0], g_sem.at[0], part, 1)
    for p in range(1, PIECES):
        for part in parts:
            send_part(g_copies[p], sg.at[p], rg.at[p], g_sem.at[p], part, 1)
    for shift in (RELAY, -RELAY):
        pl.semaphore_signal(relay_sem, inc=1, device_id=at_z(shift), device_id_type=MESH)
    rx[0] = sx[0]
    for p in range(PIECES):
        rg[p, 0] = sg[p, 0]

    spread_w = place_w[...].reshape(whole, tokens).T
    high = spread_w.astype(BF16)
    low = (spread_w - high.astype(F32)).astype(BF16)
    spread_one = place[...].astype(F32).reshape(whole, tokens).T.astype(BF16)

    for load in loads[4:]:
        load.wait()
    hidden_width = wg.shape[1]
    tile = 256
    for g in reversed(range(GROUPS)):
        members = range(g * GROUP, (g + 1) * GROUP)
        for j in members:
            if j:
                x_copies[j].wait_recv()
        rows_in = rx[g * GROUP:(g + 1) * GROUP].reshape(ROWS, width)
        span = slice(g * ROWS, (g + 1) * ROWS)
        for n in range(hidden_width // tile):
            cols = slice(n * tile, (n + 1) * tile)
            gate = jnp.dot(rows_in, wg[:, cols], preferred_element_type=F32)
            up = jnp.dot(rows_in, wu[:, cols], preferred_element_type=F32)
            sig = jax.nn.sigmoid(gate)
            activated = gate * sig
            hidden = activated * up
            act[span, cols] = activated
            rate[span, cols] = up * (sig * (1.0 + gate * (1.0 - sig)))
            hid[:, cols] = hidden.astype(BF16)
            turned = hidden.T.astype(BF16).reshape(tile // 32, 2, 16, ROWS)
            chunk = slice(n * (tile // 32), (n + 1) * (tile // 32))
            hid_t[0, chunk, :, span] = turned[:, 0]
            hid_t[1, chunk, :, span] = turned[:, 1]
        result = jnp.dot(hid[...], wd[...], preferred_element_type=F32)
        se[g * GROUP:(g + 1) * GROUP] = result.astype(BF16).reshape(GROUP, CAP, width)
    re[0] = se[0]

    c_copies = {}

    def down(p):
        for j in range(1, SLOTS):
            g_copies[p][j].wait_recv()
        grads = rg[p].reshape(whole, piece)
        lhs = hid_t[1 - c].reshape(z_count * 16, whole)
        term = jnp.dot(lhs, grads, preferred_element_type=F32)
        sc[p] = term.astype(BF16).reshape(z_count, 16, piece)
        copy = pltpu.make_async_remote_copy(
            sc.at[p], rc.at[p], c_sem.at[0, p], c_sem.at[1, p],
            device_id=(z * 2 + 1 - c, ex), device_id_type=MESH)
        copy.start()
        c_copies[p] = copy
        lhs = hid_t[c].reshape(z_count * 16, whole)
        own[p] = jnp.dot(lhs, grads, preferred_element_type=F32).reshape(z_count, 16, piece)

    def backward(g):
        span = slice(g * ROWS, (g + 1) * ROWS)
        row_grad = [rg[p, g * GROUP:(g + 1) * GROUP].reshape(ROWS, piece) for p in range(PIECES)]
        total = jnp.zeros((ROWS, width), F32)
        turn = (((1,), (1,)), ((), ()))
        for n in range(hidden_width // tile):
            cols = slice(n * tile, (n + 1) * tile)
            back = jnp.zeros((ROWS, tile), F32)
            for p in range(PIECES):
                back += lax.dot_general(
                    row_grad[p], wd[cols, p * piece:(p + 1) * piece], turn, preferred_element_type=F32)
            gate_grad = (back * rate[span, cols]).astype(BF16)
            up_grad = (back * act[span, cols]).astype(BF16)
            total += lax.dot_general(gate_grad, wg[:, cols], turn, preferred_element_type=F32)
            total += lax.dot_general(up_grad, wu[:, cols], turn, preferred_element_type=F32)
        si[g * GROUP:(g + 1) * GROUP] = total.astype(BF16).reshape(GROUP, CAP, width)
        send_part(i_copies, si, ri, i_sem, slice(g * GROUP, (g + 1) * GROUP), -1)

    hops = {}

    def partial(p, r):
        d = lax.rem(z - r + z_count, z_count)
        value = own[p, d] + rc[p, d].astype(F32)
        for child in CHILDREN.get(r, ()):
            hops[p, child].wait_recv()
            value = value + hop_r[p, HOP_AT[child]].astype(F32)
        return value

    def hop(p, r):
        i = HOP_AT[r]
        hop_s[p, i] = partial(p, r).astype(BF16)
        copy = pltpu.make_async_remote_copy(
            hop_s.at[p, i], hop_r.at[p, i], h_sem.at[0, p, i], h_sem.at[1, p, i],
            device_id=at_z(PARENT[r] - r), device_id_type=MESH)
        copy.start()
        hops[p, r] = copy

    down(0)
    pl.semaphore_wait(relay_sem, 2)
    c_copies[0].wait_recv()
    for r in LEAVES:
        hop(0, r)
    down(1)
    for part in parts:
        send_part(e_copies, se, re, e_sem, part, -1)
    backward(1)
    c_copies[1].wait_recv()
    for r in LEAVES:
        hop(1, r)
    backward(0)
    ri[0] = si[0]
    for p, r in LATER:
        hop(p, r)
    for j in range(1, SLOTS):
        e_copies[j].wait_recv()
    returned = re[...].reshape(whole, width)
    summed = jnp.dot(high, returned, preferred_element_type=F32)
    summed += jnp.dot(low, returned, preferred_element_type=F32)
    out_ref[...] = summed.astype(BF16)
    for j in range(1, SLOTS):
        i_copies[j].wait_recv()
    grad_ref[...] = jnp.dot(
        spread_one, ri[...].reshape(whole, width), preferred_element_type=F32).astype(BF16)
    for p in range(PIECES):
        down_ref[:, p * piece:(p + 1) * piece] = partial(p, 0)

    for copies in (x_copies, *g_copies, e_copies, i_copies, c_copies, hops):
        for copy in copies.values():
            copy.wait_send()


def store(*refs):
    copies = [pltpu.make_async_copy(refs[i], refs[3 + i], refs[6].at[i]) for i in range(3)]
    for copy in copies:
        copy.start()
    for copy in copies:
        copy.wait()


def local(latents, routes, gate_level, cotangent, w_gate, w_up, w_down):
    tokens, width = latents.shape
    hidden = w_gate.shape[2]
    whole = SLOTS * CAP
    z_count = lax.axis_size("dp") // 2
    block = (SLOTS, CAP, width)
    piece = width // PIECES
    sums = (PIECES, z_count, 16, piece)
    hop_count = len(HOPS)
    anywhere = pl.BlockSpec(memory_space=pl.ANY)
    in_vmem = pl.BlockSpec(memory_space=pltpu.VMEM)
    dma = pltpu.SemaphoreType.DMA
    results = pl.pallas_call(
        kernel,
        out_shape=(
            pltpu.VMEM((tokens, width), BF16),
            pltpu.VMEM((tokens, width), BF16),
            pltpu.VMEM((16, width), F32),
        ),
        in_specs=[anywhere] * 7,
        out_specs=(in_vmem,) * 3,
        scratch_shapes=[
            pltpu.VMEM(latents.shape, BF16),
            pltpu.VMEM(routes.shape[::-1], jnp.int32),
            pltpu.VMEM(gate_level.shape[::-1], jnp.int32),
            pltpu.VMEM(cotangent.shape, BF16),
            pltpu.VMEM((width, hidden), BF16),
            pltpu.VMEM((width, hidden), BF16),
            pltpu.VMEM((hidden, width), BF16),
            pltpu.VMEM((SLOTS, tokens), F32),
            pltpu.VMEM((SLOTS, tokens), F32),
            pltpu.VMEM((SLOTS, CAP, tokens), BF16),
            pltpu.VMEM((SLOTS, CAP, tokens), F32),
        ] + [pltpu.VMEM(block, BF16)] * 2 + [pltpu.VMEM((PIECES, SLOTS, CAP, piece), BF16)] * 2 + [
            pltpu.VMEM(block, BF16)] * 4 + [
            pltpu.VMEM((ROWS, hidden), BF16),
            pltpu.VMEM((2, z_count, 16, whole), BF16),
            pltpu.VMEM((whole, hidden), F32),
            pltpu.VMEM((whole, hidden), F32),
            pltpu.VMEM(sums, F32),
            pltpu.VMEM(sums, BF16),
            pltpu.VMEM(sums, BF16),
            pltpu.VMEM((PIECES, hop_count, 16, piece), BF16),
            pltpu.VMEM((PIECES, hop_count, 16, piece), BF16),
            dma((7,)), dma((2, SLOTS)), dma((PIECES, 2, SLOTS)), dma((2, SLOTS)), dma((2, SLOTS)),
            dma((2, PIECES)), dma((2, PIECES, hop_count)), pltpu.SemaphoreType.REGULAR,
        ],
        compiler_params=pltpu.CompilerParams(
            collective_id=0, has_side_effects=True, vmem_limit_bytes=56 << 20),
        name="moe",
    )(latents, routes.T, gate_level.T, cotangent, w_gate[0], w_up[0], w_down[0])
    latent_out, grad_latents, grad_down = pl.pallas_call(
        store,
        out_shape=[jax.ShapeDtypeStruct(r.shape, r.dtype) for r in results],
        in_specs=[anywhere] * 3,
        out_specs=[anywhere] * 3,
        scratch_shapes=[dma((3,))],
        name="store",
    )(*[pltpu.with_memory_space_constraint(r, pltpu.VMEM) for r in results])
    return latent_out, grad_latents, grad_down[None]


def solution(mesh):
    return jax.shard_map(
        local,
        mesh=mesh,
        in_specs=(
            P(("dp", "expert"), None),
            P(("dp", "expert"), None),
            P(("dp", "expert"), None),
            P(("dp", "expert"), None),
            P("expert", None, None),
            P("expert", None, None),
            P("expert", None, None),
        ),
        out_specs=(P(("dp", "expert"), None), P(("dp", "expert"), None), P("expert", "dp", None)),
        check_vma=False,
    )
```

```python
import jax
import jax.numpy as jnp
from jax import lax
from jax.experimental import pallas as pl
from jax.experimental.pallas import tpu as pltpu
from jax.sharding import PartitionSpec as P

CAP = 32
SIDE = 4
F32 = jnp.float32
BF16 = jnp.bfloat16
MESH = pl.DeviceIdType.MESH


def ring_distance(step):
    return min(step, SIDE - step)


PLACES = sorted(
    [(dy, dx) for dy in range(SIDE) for dx in range(SIDE)],
    key=lambda o: (ring_distance(o[0]) + ring_distance(o[1]), o),
)
SLOTS = len(PLACES)
GROUP = 8
GROUPS = SLOTS // GROUP
ROWS = GROUP * CAP

PARENT = {}
for _r, _q in {
    1: 0, 2: 1, 3: 2, 4: 0, 5: 4, 6: 5, 7: 9, 8: 9, 9: 10, 10: 0, 11: 10, 12: 10, 13: 14, 14: 10, 15: 14,
}.items():
    PARENT[_r], PARENT[-_r] = _q, -_q
PARENT[-16] = -14
CHILDREN = {}
for _r, _q in PARENT.items():
    CHILDREN.setdefault(_q, []).append(_r)
LEAVES = [-16, -15, -13, 13, 15, -7, 7, -8, 8, -6, 6, -12, 12, -11, 11, -3, 3]
PIECES = 2
INNER_NEAR = [14, -14, 5, -5, 2, -2, -9, 9]
INNER_FAR = [4, -4, 1, -1, -10, 10]
HOPS = LEAVES + INNER_NEAR + INNER_FAR
HOP_AT = {r: i for i, r in enumerate(HOPS)}
Z_NEAR = (1, -1, 2, -2)
RELAYS = (2, 4)


def kernel(
    lat_hbm, routes_hbm, level_hbm, cot_hbm, wg_hbm, wu_hbm, wd_hbm,
    out_ref, grad_ref, down_ref,
    lat, routes, level, cot, wg, wu, wd,
    key, share, place, place_w,
    sx, rx, sg, rg, se, re, si, ri,
    hid, hid_t, act, rate,
    own, sc, rc, hop_s, hop_r,
    load_sem, x_sem, g_sem, e_sem, i_sem, c_sem, h_sem, relay_sem,
):
    dp, ex = lax.axis_index("dp"), lax.axis_index("expert")
    z_count = lax.axis_size("dp") // 2
    z, c = dp // 2, lax.rem(dp, 2)
    y, x = ex // SIDE, lax.rem(ex, SIDE)

    def at_place(place_index, sign):
        dy, dx = PLACES[place_index]
        return lax.rem(y + sign * dy + SIDE, SIDE) * SIDE + lax.rem(x + sign * dx + SIDE, SIDE)

    def at_z(shift):
        return (lax.rem(z + shift + z_count, z_count) * 2 + c, ex)

    loads = [
        pltpu.make_async_copy(source, target, load_sem.at[i])
        for i, (source, target) in enumerate(
            ((routes_hbm, routes), (level_hbm, level), (lat_hbm, lat), (cot_hbm, cot),
             (wg_hbm, wg), (wu_hbm, wu), (wd_hbm, wd))
        )
    ]
    for load in loads[:4]:
        load.start()

    barrier = pltpu.get_barrier_semaphore()
    greeted = [(dp, at_place(j, 1)) for j in range(1, SLOTS)]
    greeted += [at_z(d) for d in Z_NEAR] + [(z * 2 + 1 - c, ex)]
    for device in greeted:
        pl.semaphore_signal(barrier, inc=1, device_id=device, device_id_type=MESH)

    loads[0].wait()
    loads[1].wait()

    tokens = lat.shape[0]
    lane = lax.broadcasted_iota(jnp.int32, (tokens, tokens), 1)
    row = lax.broadcasted_iota(jnp.int32, (tokens, tokens), 0)
    expert = lax.broadcasted_iota(jnp.int32, (SLOTS, tokens), 0)
    named = routes[...]
    levels = level[...].astype(F32)
    weight = levels / (levels[0:1] + levels[1:2] + levels[2:3])
    chosen_t = jnp.zeros((SLOTS, tokens), F32)
    share_t = jnp.zeros((SLOTS, tokens), F32)
    for k in range(3):
        hit = named[k:k + 1] == expert
        chosen_t = jnp.where(hit, 1.0, chosen_t)
        share_t = jnp.where(hit, weight[k:k + 1], share_t)
    share[...] = share_t
    earlier = (row < lane).astype(F32).astype(BF16)
    before = jnp.dot(chosen_t.astype(BF16), earlier, preferred_element_type=F32)
    key[...] = jnp.where(chosen_t > 0.0, before, -1.0)
    slot_of = lax.broadcasted_iota(jnp.int32, (CAP, tokens), 0).astype(F32)
    for j in range(SLOTS):
        e = at_place(j, 1)
        taken = key[pl.ds(e, 1), :] == slot_of
        place[j] = jnp.where(taken, 1.0, 0.0).astype(BF16)
        place_w[j] = jnp.where(taken, share[pl.ds(e, 1), :], 0.0)

    whole = SLOTS * CAP
    width = lat.shape[1]
    parts = [slice(g * GROUP, (g + 1) * GROUP) for g in reversed(range(GROUPS))]

    def send(source, target, sems, j, sign):
        copy = pltpu.make_async_remote_copy(
            source.at[j], target.at[j], sems.at[0, j], sems.at[1, j],
            device_id=(dp, at_place(j, sign)), device_id_type=MESH)
        copy.start()
        return copy

    def send_part(copies, source, target, sems, part, sign):
        for j in reversed(range(part.start, part.stop)):
            if j:
                copies[j] = send(source, target, sems, j, sign)

    x_copies, e_copies, i_copies = {}, {}, {}
    g_copies = [{} for _ in range(PIECES)]
    piece = width // PIECES
    loads[2].wait()
    loads[3].wait()
    for load in loads[4:]:
        load.start()
    for n, part in enumerate(parts):
        picked = place[part].reshape(ROWS, tokens)
        sx[part] = jnp.dot(picked, lat[...], preferred_element_type=F32).astype(BF16).reshape(
            GROUP, CAP, width)
        if n == 0:
            pl.semaphore_wait(barrier, len(greeted))
        send_part(x_copies, sx, rx, x_sem, part, 1)

    def relay(i):
        for shift in (RELAYS[i], -RELAYS[i]):
            pl.semaphore_signal(relay_sem.at[i], inc=1, device_id=at_z(shift), device_id_type=MESH)

    relay(0)
    for part in parts:
        picked = place[part].reshape(ROWS, tokens)
        row_weight = jnp.sum(place_w[part].reshape(ROWS, tokens), axis=1, keepdims=True)
        scaled = row_weight * jnp.dot(picked, cot[...], preferred_element_type=F32)
        scaled = scaled.astype(BF16)
        for p in range(PIECES):
            sg[p, part] = scaled[:, p * piece:(p + 1) * piece].reshape(GROUP, CAP, piece)
        send_part(g_copies[0], sg.at[0], rg.at[0], g_sem.at[0], part, 1)
    for p in range(1, PIECES):
        for part in parts:
            send_part(g_copies[p], sg.at[p], rg.at[p], g_sem.at[p], part, 1)
    pl.semaphore_wait(relay_sem.at[0], 2)
    relay(1)
    rx[0] = sx[0]
    for p in range(PIECES):
        rg[p, 0] = sg[p, 0]

    spread_w = place_w[...].reshape(whole, tokens).T
    high = spread_w.astype(BF16)
    low = (spread_w - high.astype(F32)).astype(BF16)
    spread_one = place[...].astype(F32).reshape(whole, tokens).T.astype(BF16)

    for load in loads[4:]:
        load.wait()
    hidden_width = wg.shape[1]
    tile = 256
    for g in reversed(range(GROUPS)):
        members = range(g * GROUP, (g + 1) * GROUP)
        for j in members:
            if j:
                x_copies[j].wait_recv()
        rows_in = rx[g * GROUP:(g + 1) * GROUP].reshape(ROWS, width)
        span = slice(g * ROWS, (g + 1) * ROWS)
        for n in range(hidden_width // tile):
            cols = slice(n * tile, (n + 1) * tile)
            gate = jnp.dot(rows_in, wg[:, cols], preferred_element_type=F32)
            up = jnp.dot(rows_in, wu[:, cols], preferred_element_type=F32)
            sig = jax.nn.sigmoid(gate)
            activated = gate * sig
            hidden = activated * up
            act[span, cols] = activated
            rate[span, cols] = up * (sig * (1.0 + gate * (1.0 - sig)))
            hid[:, cols] = hidden.astype(BF16)
            turned = hidden.T.astype(BF16).reshape(tile // 32, 2, 16, ROWS)
            chunk = slice(n * (tile // 32), (n + 1) * (tile // 32))
            hid_t[0, chunk, :, span] = turned[:, 0]
            hid_t[1, chunk, :, span] = turned[:, 1]
        result = jnp.dot(hid[...], wd[...], preferred_element_type=F32)
        se[g * GROUP:(g + 1) * GROUP] = result.astype(BF16).reshape(GROUP, CAP, width)
    re[0] = se[0]

    c_copies = {}

    def down(p):
        for j in range(1, SLOTS):
            g_copies[p][j].wait_recv()
        grads = rg[p].reshape(whole, piece)
        lhs = hid_t[1 - c].reshape(z_count * 16, whole)
        term = jnp.dot(lhs, grads, preferred_element_type=F32)
        sc[p] = term.astype(BF16).reshape(z_count, 16, piece)
        copy = pltpu.make_async_remote_copy(
            sc.at[p], rc.at[p], c_sem.at[0, p], c_sem.at[1, p],
            device_id=(z * 2 + 1 - c, ex), device_id_type=MESH)
        copy.start()
        c_copies[p] = copy
        lhs = hid_t[c].reshape(z_count * 16, whole)
        own[p] = jnp.dot(lhs, grads, preferred_element_type=F32).reshape(z_count, 16, piece)

    def backward(g):
        span = slice(g * ROWS, (g + 1) * ROWS)
        row_grad = [rg[p, g * GROUP:(g + 1) * GROUP].reshape(ROWS, piece) for p in range(PIECES)]
        total = jnp.zeros((ROWS, width), F32)
        turn = (((1,), (1,)), ((), ()))
        for n in range(hidden_width // tile):
            cols = slice(n * tile, (n + 1) * tile)
            back = jnp.zeros((ROWS, tile), F32)
            for p in range(PIECES):
                back += lax.dot_general(
                    row_grad[p], wd[cols, p * piece:(p + 1) * piece], turn, preferred_element_type=F32)
            gate_grad = (back * rate[span, cols]).astype(BF16)
            up_grad = (back * act[span, cols]).astype(BF16)
            total += lax.dot_general(gate_grad, wg[:, cols], turn, preferred_element_type=F32)
            total += lax.dot_general(up_grad, wu[:, cols], turn, preferred_element_type=F32)
        si[g * GROUP:(g + 1) * GROUP] = total.astype(BF16).reshape(GROUP, CAP, width)
        send_part(i_copies, si, ri, i_sem, slice(g * GROUP, (g + 1) * GROUP), -1)

    hops = {}

    def partial(p, r):
        d = lax.rem(z - r + z_count, z_count)
        value = own[p, d] + rc[p, d].astype(F32)
        for child in CHILDREN.get(r, ()):
            hops[p, child].wait_recv()
            value = value + hop_r[p, HOP_AT[child]].astype(F32)
        return value

    def hop(p, r):
        i = HOP_AT[r]
        hop_s[p, i] = partial(p, r).astype(BF16)
        copy = pltpu.make_async_remote_copy(
            hop_s.at[p, i], hop_r.at[p, i], h_sem.at[0, p, i], h_sem.at[1, p, i],
            device_id=at_z(PARENT[r] - r), device_id_type=MESH)
        copy.start()
        hops[p, r] = copy

    down(0)
    pl.semaphore_wait(relay_sem.at[1], 2)
    c_copies[0].wait_recv()
    for r in LEAVES:
        hop(0, r)
    down(1)
    for part in parts:
        send_part(e_copies, se, re, e_sem, part, -1)
    c_copies[1].wait_recv()
    for r in LEAVES:
        hop(1, r)
    for p in range(PIECES):
        for r in INNER_NEAR:
            hop(p, r)
    backward(1)
    for r in INNER_FAR:
        hop(0, r)
    backward(0)
    ri[0] = si[0]
    for r in INNER_FAR:
        hop(1, r)
    for copies in (x_copies, *g_copies, c_copies):
        for copy in copies.values():
            copy.wait_send()
    for p in range(PIECES):
        for r in LEAVES + INNER_NEAR:
            hops[p, r].wait_send()
    for j in range(1, SLOTS):
        e_copies[j].wait_recv()
    returned = re[...].reshape(whole, width)
    summed = jnp.dot(high, returned, preferred_element_type=F32)
    summed += jnp.dot(low, returned, preferred_element_type=F32)
    out_ref[...] = summed.astype(BF16)
    for j in range(1, SLOTS):
        i_copies[j].wait_recv()
    grad_ref[...] = jnp.dot(
        spread_one, ri[...].reshape(whole, width), preferred_element_type=F32).astype(BF16)
    for copies in (e_copies, i_copies):
        for copy in copies.values():
            copy.wait_send()
    for p in range(PIECES):
        down_ref[:, p * piece:(p + 1) * piece] = partial(p, 0)
    for p in range(PIECES):
        for r in INNER_FAR:
            hops[p, r].wait_send()


def store(*refs):
    copies = [pltpu.make_async_copy(refs[i], refs[3 + i], refs[6].at[i]) for i in range(3)]
    for copy in copies:
        copy.start()
    for copy in copies:
        copy.wait()


def local(latents, routes, gate_level, cotangent, w_gate, w_up, w_down):
    tokens, width = latents.shape
    hidden = w_gate.shape[2]
    whole = SLOTS * CAP
    z_count = lax.axis_size("dp") // 2
    block = (SLOTS, CAP, width)
    piece = width // PIECES
    sums = (PIECES, z_count, 16, piece)
    hop_count = len(HOPS)
    anywhere = pl.BlockSpec(memory_space=pl.ANY)
    in_vmem = pl.BlockSpec(memory_space=pltpu.VMEM)
    dma = pltpu.SemaphoreType.DMA
    results = pl.pallas_call(
        kernel,
        out_shape=(
            pltpu.VMEM((tokens, width), BF16),
            pltpu.VMEM((tokens, width), BF16),
            pltpu.VMEM((16, width), F32),
        ),
        in_specs=[anywhere] * 7,
        out_specs=(in_vmem,) * 3,
        scratch_shapes=[
            pltpu.VMEM(latents.shape, BF16),
            pltpu.VMEM(routes.shape[::-1], jnp.int32),
            pltpu.VMEM(gate_level.shape[::-1], jnp.int32),
            pltpu.VMEM(cotangent.shape, BF16),
            pltpu.VMEM((width, hidden), BF16),
            pltpu.VMEM((width, hidden), BF16),
            pltpu.VMEM((hidden, width), BF16),
            pltpu.VMEM((SLOTS, tokens), F32),
            pltpu.VMEM((SLOTS, tokens), F32),
            pltpu.VMEM((SLOTS, CAP, tokens), BF16),
            pltpu.VMEM((SLOTS, CAP, tokens), F32),
        ] + [pltpu.VMEM(block, BF16)] * 2 + [pltpu.VMEM((PIECES, SLOTS, CAP, piece), BF16)] * 2 + [
            pltpu.VMEM(block, BF16)] * 4 + [
            pltpu.VMEM((ROWS, hidden), BF16),
            pltpu.VMEM((2, z_count, 16, whole), BF16),
            pltpu.VMEM((whole, hidden), F32),
            pltpu.VMEM((whole, hidden), F32),
            pltpu.VMEM(sums, F32),
            pltpu.VMEM(sums, BF16),
            pltpu.VMEM(sums, BF16),
            pltpu.VMEM((PIECES, hop_count, 16, piece), BF16),
            pltpu.VMEM((PIECES, hop_count, 16, piece), BF16),
            dma((7,)), dma((2, SLOTS)), dma((PIECES, 2, SLOTS)), dma((2, SLOTS)), dma((2, SLOTS)),
            dma((2, PIECES)), dma((2, PIECES, hop_count)), pltpu.SemaphoreType.REGULAR((2,)),
        ],
        compiler_params=pltpu.CompilerParams(
            collective_id=0, has_side_effects=True, vmem_limit_bytes=56 << 20),
        name="moe",
    )(latents, routes.T, gate_level.T, cotangent, w_gate[0], w_up[0], w_down[0])
    latent_out, grad_latents, grad_down = pl.pallas_call(
        store,
        out_shape=[jax.ShapeDtypeStruct(r.shape, r.dtype) for r in results],
        in_specs=[anywhere] * 3,
        out_specs=[anywhere] * 3,
        scratch_shapes=[dma((3,))],
        name="store",
    )(*[pltpu.with_memory_space_constraint(r, pltpu.VMEM) for r in results])
    return latent_out, grad_latents, grad_down[None]


def solution(mesh):
    return jax.shard_map(
        local,
        mesh=mesh,
        in_specs=(
            P(("dp", "expert"), None),
            P(("dp", "expert"), None),
            P(("dp", "expert"), None),
            P(("dp", "expert"), None),
            P("expert", None, None),
            P("expert", None, None),
            P("expert", None, None),
        ),
        out_specs=(P(("dp", "expert"), None), P(("dp", "expert"), None), P("expert", "dp", None)),
        check_vma=False,
    )
```

```python
import jax
import jax.numpy as jnp
from jax import lax
from jax.experimental import pallas as pl
from jax.experimental.pallas import tpu as pltpu
from jax.sharding import PartitionSpec as P

CAP = 32
SIDE = 4
F32 = jnp.float32
BF16 = jnp.bfloat16
MESH = pl.DeviceIdType.MESH


def ring_distance(step):
    return min(step, SIDE - step)


PLACES = sorted(
    [(dy, dx) for dy in range(SIDE) for dx in range(SIDE)],
    key=lambda o: (ring_distance(o[0]) + ring_distance(o[1]), o),
)
SLOTS = len(PLACES)
GROUP = 8
GROUPS = SLOTS // GROUP
ROWS = GROUP * CAP

PARENT = {}
for _r, _q in {
    1: 0, 2: 1, 3: 2, 4: 0, 5: 4, 6: 5, 7: 9, 8: 9, 9: 10, 10: 0, 11: 10, 12: 10, 13: 14, 14: 10, 15: 14,
}.items():
    PARENT[_r], PARENT[-_r] = _q, -_q
PARENT[-16] = -14
CHILDREN = {}
for _r, _q in PARENT.items():
    CHILDREN.setdefault(_q, []).append(_r)
LEAVES = [-16, -15, -13, 13, 15, -7, 7, -8, 8, -6, 6, -12, 12, -11, 11, -3, 3]
PIECES = 2
INNER_NEAR = [14, -14, 5, -5, 2, -2, -9, 9]
INNER_FAR = [4, -4, 1, -1, -10, 10]
HOPS = [r for q in CHILDREN for r in CHILDREN[q]]
HOP_AT = {r: i for i, r in enumerate(HOPS)}
PARENT_AT = {q: i for i, q in enumerate(CHILDREN)}
Z_NEAR = (1, -1, 2, -2)
RELAYS = (2, 4)


def kernel(
    lat_hbm, routes_hbm, level_hbm, cot_hbm, wg_hbm, wu_hbm, wd_hbm,
    out_ref, grad_ref, down_ref,
    lat, routes, level, cot, wg, wu, wd,
    key, share, place, place_w,
    sx, rx, sg, rg, se, re, si, ri,
    hid, hid_t, act, rate,
    own, sc, rc, hop_s, hop_r,
    load_sem, x_sem, g_sem, e_sem, i_sem, c_sem, hop_sem, hop_sent, relay_sem,
):
    dp, ex = lax.axis_index("dp"), lax.axis_index("expert")
    z_count = lax.axis_size("dp") // 2
    z, c = dp // 2, lax.rem(dp, 2)
    y, x = ex // SIDE, lax.rem(ex, SIDE)

    def at_place(place_index, sign):
        dy, dx = PLACES[place_index]
        return lax.rem(y + sign * dy + SIDE, SIDE) * SIDE + lax.rem(x + sign * dx + SIDE, SIDE)

    def at_z(shift):
        return (lax.rem(z + shift + z_count, z_count) * 2 + c, ex)

    loads = [
        pltpu.make_async_copy(source, target, load_sem.at[i])
        for i, (source, target) in enumerate(
            ((routes_hbm, routes), (level_hbm, level), (lat_hbm, lat), (cot_hbm, cot),
             (wg_hbm, wg), (wu_hbm, wu), (wd_hbm, wd))
        )
    ]
    for load in loads[:4]:
        load.start()

    barrier = pltpu.get_barrier_semaphore()
    greeted = [(dp, at_place(j, 1)) for j in range(1, SLOTS)]
    greeted += [at_z(d) for d in Z_NEAR] + [(z * 2 + 1 - c, ex)]
    for device in greeted:
        pl.semaphore_signal(barrier, inc=1, device_id=device, device_id_type=MESH)

    loads[0].wait()
    loads[1].wait()

    tokens = lat.shape[0]
    lane = lax.broadcasted_iota(jnp.int32, (tokens, tokens), 1)
    row = lax.broadcasted_iota(jnp.int32, (tokens, tokens), 0)
    expert = lax.broadcasted_iota(jnp.int32, (SLOTS, tokens), 0)
    named = routes[...]
    levels = level[...].astype(F32)
    weight = levels / (levels[0:1] + levels[1:2] + levels[2:3])
    chosen_t = jnp.zeros((SLOTS, tokens), F32)
    share_t = jnp.zeros((SLOTS, tokens), F32)
    for k in range(3):
        hit = named[k:k + 1] == expert
        chosen_t = jnp.where(hit, 1.0, chosen_t)
        share_t = jnp.where(hit, weight[k:k + 1], share_t)
    share[...] = share_t
    earlier = (row < lane).astype(F32).astype(BF16)
    before = jnp.dot(chosen_t.astype(BF16), earlier, preferred_element_type=F32)
    key[...] = jnp.where(chosen_t > 0.0, before, -1.0)
    slot_of = lax.broadcasted_iota(jnp.int32, (CAP, tokens), 0).astype(F32)
    for j in range(SLOTS):
        e = at_place(j, 1)
        taken = key[pl.ds(e, 1), :] == slot_of
        place[j] = jnp.where(taken, 1.0, 0.0).astype(BF16)
        place_w[j] = jnp.where(taken, share[pl.ds(e, 1), :], 0.0)

    whole = SLOTS * CAP
    width = lat.shape[1]
    parts = [slice(g * GROUP, (g + 1) * GROUP) for g in reversed(range(GROUPS))]

    def send(source, target, send_sem, recv_sem, part, sign):
        for j in reversed(range(max(part.start, 1), part.stop)):
            pltpu.make_async_remote_copy(
                source.at[j], target.at[j], send_sem, recv_sem,
                device_id=(dp, at_place(j, sign)), device_id_type=MESH).start()

    def bulk(source, target, send_sem, recv_sem):
        return pltpu.make_async_remote_copy(
            source, target, send_sem, recv_sem,
            device_id=(dp, at_place(1, 1)), device_id_type=MESH)

    def sent(source, send_sem, recv_sem):
        bulk(source.at[1:], source.at[1:], send_sem, recv_sem).wait_send()

    def arrived(target, send_sem, recv_sem, part):
        rows = target.at[max(part.start, 1):part.stop]
        bulk(rows, rows, send_sem, recv_sem).wait_recv()

    every = slice(0, SLOTS)
    piece = width // PIECES
    loads[2].wait()
    loads[3].wait()
    for load in loads[4:]:
        load.start()
    for n, part in enumerate(parts):
        picked = place[part].reshape(ROWS, tokens)
        sx[part] = jnp.dot(picked, lat[...], preferred_element_type=F32).astype(BF16).reshape(
            GROUP, CAP, width)
        if n == 0:
            pl.semaphore_wait(barrier, len(greeted))
        send(sx, rx, x_sem.at[0], x_sem.at[1 + n], part, 1)

    def relay(i):
        for shift in (RELAYS[i], -RELAYS[i]):
            pl.semaphore_signal(relay_sem.at[i], inc=1, device_id=at_z(shift), device_id_type=MESH)

    relay(0)
    for part in parts:
        picked = place[part].reshape(ROWS, tokens)
        row_weight = jnp.sum(place_w[part].reshape(ROWS, tokens), axis=1, keepdims=True)
        scaled = row_weight * jnp.dot(picked, cot[...], preferred_element_type=F32)
        scaled = scaled.astype(BF16)
        for p in range(PIECES):
            sg[p, part] = scaled[:, p * piece:(p + 1) * piece].reshape(GROUP, CAP, piece)
        send(sg.at[0], rg.at[0], g_sem.at[0, 0], g_sem.at[1, 0], part, 1)
    for p in range(1, PIECES):
        send(sg.at[p], rg.at[p], g_sem.at[0, p], g_sem.at[1, p], every, 1)
    pl.semaphore_wait(relay_sem.at[0], 2)
    relay(1)
    rx[0] = sx[0]
    for p in range(PIECES):
        rg[p, 0] = sg[p, 0]

    spread_w = place_w[...].reshape(whole, tokens).T
    high = spread_w.astype(BF16)
    low = (spread_w - high.astype(F32)).astype(BF16)
    spread_one = place[...].astype(F32).reshape(whole, tokens).T.astype(BF16)

    for load in loads[4:]:
        load.wait()
    hidden_width = wg.shape[1]
    tile = 256
    for g in reversed(range(GROUPS)):
        n = GROUPS - 1 - g
        arrived(rx, x_sem.at[0], x_sem.at[1 + n], parts[n])
        rows_in = rx[g * GROUP:(g + 1) * GROUP].reshape(ROWS, width)
        span = slice(g * ROWS, (g + 1) * ROWS)
        for n in range(hidden_width // tile):
            cols = slice(n * tile, (n + 1) * tile)
            gate = jnp.dot(rows_in, wg[:, cols], preferred_element_type=F32)
            up = jnp.dot(rows_in, wu[:, cols], preferred_element_type=F32)
            sig = jax.nn.sigmoid(gate)
            activated = gate * sig
            hidden = activated * up
            act[span, cols] = activated
            rate[span, cols] = up * (sig * (1.0 + gate * (1.0 - sig)))
            hid[:, cols] = hidden.astype(BF16)
            turned = hidden.T.astype(BF16).reshape(tile // 32, 2, 16, ROWS)
            chunk = slice(n * (tile // 32), (n + 1) * (tile // 32))
            hid_t[0, chunk, :, span] = turned[:, 0]
            hid_t[1, chunk, :, span] = turned[:, 1]
        result = jnp.dot(hid[...], wd[...], preferred_element_type=F32)
        se[g * GROUP:(g + 1) * GROUP] = result.astype(BF16).reshape(GROUP, CAP, width)
    re[0] = se[0]

    c_copies = {}

    def down(p):
        arrived(rg.at[p], g_sem.at[0, p], g_sem.at[1, p], every)
        grads = rg[p].reshape(whole, piece)
        lhs = hid_t[1 - c].reshape(z_count * 16, whole)
        term = jnp.dot(lhs, grads, preferred_element_type=F32)
        sc[p] = term.astype(BF16).reshape(z_count, 16, piece)
        copy = pltpu.make_async_remote_copy(
            sc.at[p], rc.at[p], c_sem.at[0, p], c_sem.at[1, p],
            device_id=(z * 2 + 1 - c, ex), device_id_type=MESH)
        copy.start()
        c_copies[p] = copy
        lhs = hid_t[c].reshape(z_count * 16, whole)
        own[p] = jnp.dot(lhs, grads, preferred_element_type=F32).reshape(z_count, 16, piece)

    def backward(g):
        span = slice(g * ROWS, (g + 1) * ROWS)
        row_grad = [rg[p, g * GROUP:(g + 1) * GROUP].reshape(ROWS, piece) for p in range(PIECES)]
        total = jnp.zeros((ROWS, width), F32)
        turn = (((1,), (1,)), ((), ()))
        for n in range(hidden_width // tile):
            cols = slice(n * tile, (n + 1) * tile)
            back = jnp.zeros((ROWS, tile), F32)
            for p in range(PIECES):
                back += lax.dot_general(
                    row_grad[p], wd[cols, p * piece:(p + 1) * piece], turn, preferred_element_type=F32)
            gate_grad = (back * rate[span, cols]).astype(BF16)
            up_grad = (back * act[span, cols]).astype(BF16)
            total += lax.dot_general(gate_grad, wg[:, cols], turn, preferred_element_type=F32)
            total += lax.dot_general(up_grad, wu[:, cols], turn, preferred_element_type=F32)
        si[g * GROUP:(g + 1) * GROUP] = total.astype(BF16).reshape(GROUP, CAP, width)
        send(si, ri, i_sem.at[0], i_sem.at[1], slice(g * GROUP, (g + 1) * GROUP), -1)

    def partial(p, r):
        d = lax.rem(z - r + z_count, z_count)
        value = own[p, d] + rc[p, d].astype(F32)
        if r in CHILDREN:
            first = HOP_AT[CHILDREN[r][0]]
            last = first + len(CHILDREN[r])
            rows = hop_r.at[p, first:last]
            bulk(rows, rows, hop_sent, hop_sem.at[p, PARENT_AT[r]]).wait_recv()
            for i in range(first, last):
                value = value + hop_r[p, i].astype(F32)
        return value

    def hop(p, r):
        i = HOP_AT[r]
        hop_s[p, i] = partial(p, r).astype(BF16)
        pltpu.make_async_remote_copy(
            hop_s.at[p, i], hop_r.at[p, i], hop_sent, hop_sem.at[p, PARENT_AT[PARENT[r]]],
            device_id=at_z(PARENT[r] - r), device_id_type=MESH).start()

    down(0)
    pl.semaphore_wait(relay_sem.at[1], 2)
    c_copies[0].wait_recv()
    for r in LEAVES:
        hop(0, r)
    down(1)
    send(se, re, e_sem.at[0], e_sem.at[1], every, -1)
    c_copies[1].wait_recv()
    for r in LEAVES:
        hop(1, r)
    for p in range(PIECES):
        for r in INNER_NEAR:
            hop(p, r)
    backward(1)
    for r in INNER_FAR:
        hop(0, r)
    backward(0)
    ri[0] = si[0]
    for r in INNER_FAR:
        hop(1, r)
    sent(sx, x_sem.at[0], x_sem.at[1])
    for p in range(PIECES):
        sent(sg.at[p], g_sem.at[0, p], g_sem.at[1, p])
        c_copies[p].wait_send()
    arrived(re, e_sem.at[0], e_sem.at[1], every)
    returned = re[...].reshape(whole, width)
    summed = jnp.dot(high, returned, preferred_element_type=F32)
    summed += jnp.dot(low, returned, preferred_element_type=F32)
    out_ref[...] = summed.astype(BF16)
    arrived(ri, i_sem.at[0], i_sem.at[1], every)
    grad_ref[...] = jnp.dot(
        spread_one, ri[...].reshape(whole, width), preferred_element_type=F32).astype(BF16)
    sent(se, e_sem.at[0], e_sem.at[1])
    sent(si, i_sem.at[0], i_sem.at[1])
    for p in range(PIECES):
        down_ref[:, p * piece:(p + 1) * piece] = partial(p, 0)
    bulk(hop_s, hop_s, hop_sent, hop_sem.at[0, 0]).wait_send()


def store(*refs):
    copies = [pltpu.make_async_copy(refs[i], refs[3 + i], refs[6].at[i]) for i in range(3)]
    for copy in copies:
        copy.start()
    for copy in copies:
        copy.wait()


def local(latents, routes, gate_level, cotangent, w_gate, w_up, w_down):
    tokens, width = latents.shape
    hidden = w_gate.shape[2]
    whole = SLOTS * CAP
    z_count = lax.axis_size("dp") // 2
    block = (SLOTS, CAP, width)
    piece = width // PIECES
    sums = (PIECES, z_count, 16, piece)
    hop_count = len(HOPS)
    anywhere = pl.BlockSpec(memory_space=pl.ANY)
    in_vmem = pl.BlockSpec(memory_space=pltpu.VMEM)
    dma = pltpu.SemaphoreType.DMA
    results = pl.pallas_call(
        kernel,
        out_shape=(
            pltpu.VMEM((tokens, width), BF16),
            pltpu.VMEM((tokens, width), BF16),
            pltpu.VMEM((16, width), F32),
        ),
        in_specs=[anywhere] * 7,
        out_specs=(in_vmem,) * 3,
        scratch_shapes=[
            pltpu.VMEM(latents.shape, BF16),
            pltpu.VMEM(routes.shape[::-1], jnp.int32),
            pltpu.VMEM(gate_level.shape[::-1], jnp.int32),
            pltpu.VMEM(cotangent.shape, BF16),
            pltpu.VMEM((width, hidden), BF16),
            pltpu.VMEM((width, hidden), BF16),
            pltpu.VMEM((hidden, width), BF16),
            pltpu.VMEM((SLOTS, tokens), F32),
            pltpu.VMEM((SLOTS, tokens), F32),
            pltpu.VMEM((SLOTS, CAP, tokens), BF16),
            pltpu.VMEM((SLOTS, CAP, tokens), F32),
        ] + [pltpu.VMEM(block, BF16)] * 2 + [pltpu.VMEM((PIECES, SLOTS, CAP, piece), BF16)] * 2 + [
            pltpu.VMEM(block, BF16)] * 4 + [
            pltpu.VMEM((ROWS, hidden), BF16),
            pltpu.VMEM((2, z_count, 16, whole), BF16),
            pltpu.VMEM((whole, hidden), F32),
            pltpu.VMEM((whole, hidden), F32),
            pltpu.VMEM(sums, F32),
            pltpu.VMEM(sums, BF16),
            pltpu.VMEM(sums, BF16),
            pltpu.VMEM((PIECES, hop_count, 16, piece), BF16),
            pltpu.VMEM((PIECES, hop_count, 16, piece), BF16),
            dma((7,)), dma((1 + GROUPS,)), dma((2, PIECES)), dma((2,)), dma((2,)),
            dma((2, PIECES)), dma((PIECES, len(CHILDREN))), dma, pltpu.SemaphoreType.REGULAR((2,)),
        ],
        compiler_params=pltpu.CompilerParams(
            collective_id=0, has_side_effects=True, vmem_limit_bytes=56 << 20),
        name="moe",
    )(latents, routes.T, gate_level.T, cotangent, w_gate[0], w_up[0], w_down[0])
    latent_out, grad_latents, grad_down = pl.pallas_call(
        store,
        out_shape=[jax.ShapeDtypeStruct(r.shape, r.dtype) for r in results],
        in_specs=[anywhere] * 3,
        out_specs=[anywhere] * 3,
        scratch_shapes=[dma((3,))],
        name="store",
    )(*[pltpu.with_memory_space_constraint(r, pltpu.VMEM) for r in results])
    return latent_out, grad_latents, grad_down[None]


def solution(mesh):
    return jax.shard_map(
        local,
        mesh=mesh,
        in_specs=(
            P(("dp", "expert"), None),
            P(("dp", "expert"), None),
            P(("dp", "expert"), None),
            P(("dp", "expert"), None),
            P("expert", None, None),
            P("expert", None, None),
            P("expert", None, None),
        ),
        out_specs=(P(("dp", "expert"), None), P(("dp", "expert"), None), P("expert", "dp", None)),
        check_vma=False,
    )
```

```python
import jax
import jax.numpy as jnp
from jax import lax
from jax.experimental import pallas as pl
from jax.experimental.pallas import tpu as pltpu
from jax.sharding import PartitionSpec as P

CAP = 32
SIDE = 4
F32 = jnp.float32
BF16 = jnp.bfloat16
MESH = pl.DeviceIdType.MESH


def ring_distance(step):
    return min(step, SIDE - step)


PLACES = sorted(
    [(dy, dx) for dy in range(SIDE) for dx in range(SIDE)],
    key=lambda o: (ring_distance(o[0]) + ring_distance(o[1]), o),
)
SLOTS = len(PLACES)
GROUP = 8
GROUPS = SLOTS // GROUP
ROWS = GROUP * CAP

PARENT = {}
for _r, _q in {
    1: 0, 2: 1, 3: 2, 4: 0, 5: 4, 6: 5, 7: 9, 8: 9, 9: 10, 10: 0, 11: 10, 12: 10, 13: 14, 14: 10, 15: 14,
}.items():
    PARENT[_r], PARENT[-_r] = _q, -_q
PARENT[-16] = -14
CHILDREN = {}
for _r, _q in PARENT.items():
    CHILDREN.setdefault(_q, []).append(_r)
LEAVES = [-16, -15, -13, 13, 15, -7, 7, -8, 8, -6, 6, -12, 12, -11, 11, -3, 3]
PIECES = 2
INNER_NEAR = [14, -14, 5, -5, 2, -2, -9, 9]
INNER_FAR = [4, -4, 1, -1, -10, 10]
HOPS = [r for q in CHILDREN for r in CHILDREN[q]]
HOP_AT = {r: i for i, r in enumerate(HOPS)}
PARENT_AT = {q: i for i, q in enumerate(CHILDREN)}
Z_NEAR = (1, -1, 2, -2)
RELAYS = (2, 4)


def kernel(
    lat_hbm, routes_hbm, level_hbm, cot_hbm, wg_hbm, wu_hbm, wd_hbm,
    out_ref, grad_ref, down_ref,
    lat, routes, level, cot, wg, wu, wd,
    key, share, place, place_w,
    sx, rx, sg, rg, se, re, si, ri,
    hid, hid_t, act, rate,
    own, sc, rc, hop_s, hop_r,
    load_sem, x_sem, g_sem, e_sem, i_sem, c_sem, hop_sem, hop_sent, relay_sem,
):
    dp, ex = lax.axis_index("dp"), lax.axis_index("expert")
    z_count = lax.axis_size("dp") // 2
    z, c = dp // 2, lax.rem(dp, 2)
    y, x = ex // SIDE, lax.rem(ex, SIDE)

    def at_place(place_index, sign):
        dy, dx = PLACES[place_index]
        return lax.rem(y + sign * dy + SIDE, SIDE) * SIDE + lax.rem(x + sign * dx + SIDE, SIDE)

    def at_z(shift):
        return (lax.rem(z + shift + z_count, z_count) * 2 + c, ex)

    loads = [
        pltpu.make_async_copy(source, target, load_sem.at[i])
        for i, (source, target) in enumerate(
            ((routes_hbm, routes), (level_hbm, level), (lat_hbm, lat), (cot_hbm, cot),
             (wg_hbm, wg), (wu_hbm, wu), (wd_hbm, wd))
        )
    ]
    for load in loads[:4]:
        load.start()

    barrier = pltpu.get_barrier_semaphore()
    greeted = [(dp, at_place(j, 1)) for j in range(1, SLOTS)]
    greeted += [at_z(d) for d in Z_NEAR] + [(z * 2 + 1 - c, ex)]
    for device in greeted:
        pl.semaphore_signal(barrier, inc=1, device_id=device, device_id_type=MESH)

    loads[0].wait()
    loads[1].wait()

    tokens = lat.shape[0]
    lane = lax.broadcasted_iota(jnp.int32, (tokens, tokens), 1)
    row = lax.broadcasted_iota(jnp.int32, (tokens, tokens), 0)
    expert = lax.broadcasted_iota(jnp.int32, (SLOTS, tokens), 0)
    named = routes[...]
    levels = level[...].astype(F32)
    weight = levels / (levels[0:1] + levels[1:2] + levels[2:3])
    chosen_t = jnp.zeros((SLOTS, tokens), F32)
    share_t = jnp.zeros((SLOTS, tokens), F32)
    for k in range(3):
        hit = named[k:k + 1] == expert
        chosen_t = jnp.where(hit, 1.0, chosen_t)
        share_t = jnp.where(hit, weight[k:k + 1], share_t)
    share[...] = share_t
    earlier = (row < lane).astype(F32).astype(BF16)
    before = jnp.dot(chosen_t.astype(BF16), earlier, preferred_element_type=F32)
    key[...] = jnp.where(chosen_t > 0.0, before, -1.0)
    slot_of = lax.broadcasted_iota(jnp.int32, (CAP, tokens), 0).astype(F32)
    for j in range(SLOTS):
        e = at_place(j, 1)
        taken = key[pl.ds(e, 1), :] == slot_of
        place[j] = jnp.where(taken, 1.0, 0.0).astype(BF16)
        place_w[j] = jnp.where(taken, share[pl.ds(e, 1), :], 0.0)

    whole = SLOTS * CAP
    width = lat.shape[1]
    parts = [slice(g * GROUP, (g + 1) * GROUP) for g in reversed(range(GROUPS))]

    def send(source, target, send_sem, recv_sem, part, sign):
        for j in reversed(range(max(part.start, 1), part.stop)):
            pltpu.make_async_remote_copy(
                source.at[j], target.at[j], send_sem, recv_sem,
                device_id=(dp, at_place(j, sign)), device_id_type=MESH).start()

    def bulk(source, target, send_sem, recv_sem):
        return pltpu.make_async_remote_copy(
            source, target, send_sem, recv_sem,
            device_id=(dp, at_place(1, 1)), device_id_type=MESH)

    def sent(source, send_sem, recv_sem):
        bulk(source.at[1:], source.at[1:], send_sem, recv_sem).wait_send()

    def arrived(target, send_sem, recv_sem, part):
        rows = target.at[max(part.start, 1):part.stop]
        bulk(rows, rows, send_sem, recv_sem).wait_recv()

    every = slice(0, SLOTS)
    piece = width // PIECES
    loads[2].wait()
    loads[3].wait()
    for load in loads[4:]:
        load.start()
    for n, part in enumerate(parts):
        picked = place[part].reshape(ROWS, tokens)
        sx[part] = jnp.dot(picked, lat[...], preferred_element_type=F32).astype(BF16).reshape(
            GROUP, CAP, width)
        if n == 0:
            pl.semaphore_wait(barrier, len(greeted))
        send(sx, rx, x_sem.at[0], x_sem.at[1 + n], part, 1)

    def relay(i):
        for shift in (RELAYS[i], -RELAYS[i]):
            pl.semaphore_signal(relay_sem.at[i], inc=1, device_id=at_z(shift), device_id_type=MESH)

    relay(0)
    for part in parts:
        picked = place[part].reshape(ROWS, tokens)
        row_weight = jnp.sum(place_w[part].reshape(ROWS, tokens), axis=1, keepdims=True)
        scaled = row_weight * jnp.dot(picked, cot[...], preferred_element_type=F32)
        scaled = scaled.astype(BF16)
        for p in range(PIECES):
            sg[p, part] = scaled[:, p * piece:(p + 1) * piece].reshape(GROUP, CAP, piece)
        send(sg.at[0], rg.at[0], g_sem.at[0, 0], g_sem.at[1, 0], part, 1)
    for p in range(1, PIECES):
        send(sg.at[p], rg.at[p], g_sem.at[0, p], g_sem.at[1, p], every, 1)
    pl.semaphore_wait(relay_sem.at[0], 2)
    relay(1)
    rx[0] = sx[0]
    for p in range(PIECES):
        rg[p, 0] = sg[p, 0]

    for load in loads[4:]:
        load.wait()
    hidden_width = wg.shape[1]
    tile = 256
    for g in reversed(range(GROUPS)):
        n = GROUPS - 1 - g
        arrived(rx, x_sem.at[0], x_sem.at[1 + n], parts[n])
        rows_in = rx[g * GROUP:(g + 1) * GROUP].reshape(ROWS, width)
        span = slice(g * ROWS, (g + 1) * ROWS)
        for n in range(hidden_width // tile):
            cols = slice(n * tile, (n + 1) * tile)
            gate = jnp.dot(rows_in, wg[:, cols], preferred_element_type=F32)
            up = jnp.dot(rows_in, wu[:, cols], preferred_element_type=F32)
            sig = jax.nn.sigmoid(gate)
            activated = gate * sig
            hidden = activated * up
            act[span, cols] = activated
            rate[span, cols] = up * (sig * (1.0 + gate * (1.0 - sig)))
            hid[:, cols] = hidden.astype(BF16)
            turned = hidden.T.astype(BF16).reshape(tile // 32, 2, 16, ROWS)
            chunk = slice(n * (tile // 32), (n + 1) * (tile // 32))
            hid_t[0, chunk, :, span] = turned[:, 0]
            hid_t[1, chunk, :, span] = turned[:, 1]
        result = jnp.dot(hid[...], wd[...], preferred_element_type=F32)
        se[g * GROUP:(g + 1) * GROUP] = result.astype(BF16).reshape(GROUP, CAP, width)
    re[0] = se[0]

    c_copies = {}

    def down(p):
        arrived(rg.at[p], g_sem.at[0, p], g_sem.at[1, p], every)
        grads = rg[p].reshape(whole, piece)
        lhs = hid_t[1 - c].reshape(z_count * 16, whole)
        term = jnp.dot(lhs, grads, preferred_element_type=F32)
        sc[p] = term.astype(BF16).reshape(z_count, 16, piece)
        copy = pltpu.make_async_remote_copy(
            sc.at[p], rc.at[p], c_sem.at[0, p], c_sem.at[1, p],
            device_id=(z * 2 + 1 - c, ex), device_id_type=MESH)
        copy.start()
        c_copies[p] = copy
        lhs = hid_t[c].reshape(z_count * 16, whole)
        own[p] = jnp.dot(lhs, grads, preferred_element_type=F32).reshape(z_count, 16, piece)

    def backward(g):
        span = slice(g * ROWS, (g + 1) * ROWS)
        row_grad = [rg[p, g * GROUP:(g + 1) * GROUP].reshape(ROWS, piece) for p in range(PIECES)]
        total = jnp.zeros((ROWS, width), F32)
        turn = (((1,), (1,)), ((), ()))
        for n in range(hidden_width // tile):
            cols = slice(n * tile, (n + 1) * tile)
            back = jnp.zeros((ROWS, tile), F32)
            for p in range(PIECES):
                back += lax.dot_general(
                    row_grad[p], wd[cols, p * piece:(p + 1) * piece], turn, preferred_element_type=F32)
            gate_grad = (back * rate[span, cols]).astype(BF16)
            up_grad = (back * act[span, cols]).astype(BF16)
            total += lax.dot_general(gate_grad, wg[:, cols], turn, preferred_element_type=F32)
            total += lax.dot_general(up_grad, wu[:, cols], turn, preferred_element_type=F32)
        si[g * GROUP:(g + 1) * GROUP] = total.astype(BF16).reshape(GROUP, CAP, width)
        send(si, ri, i_sem.at[0], i_sem.at[1], slice(g * GROUP, (g + 1) * GROUP), -1)

    def partial(p, r):
        d = lax.rem(z - r + z_count, z_count)
        value = own[p, d] + rc[p, d].astype(F32)
        if r in CHILDREN:
            first = HOP_AT[CHILDREN[r][0]]
            last = first + len(CHILDREN[r])
            rows = hop_r.at[p, first:last]
            bulk(rows, rows, hop_sent, hop_sem.at[p, PARENT_AT[r]]).wait_recv()
            for i in range(first, last):
                value = value + hop_r[p, i].astype(F32)
        return value

    def hop(p, r):
        i = HOP_AT[r]
        hop_s[p, i] = partial(p, r).astype(BF16)
        pltpu.make_async_remote_copy(
            hop_s.at[p, i], hop_r.at[p, i], hop_sent, hop_sem.at[p, PARENT_AT[PARENT[r]]],
            device_id=at_z(PARENT[r] - r), device_id_type=MESH).start()

    down(0)
    pl.semaphore_wait(relay_sem.at[1], 2)
    c_copies[0].wait_recv()
    for r in LEAVES:
        hop(0, r)
    down(1)
    send(se, re, e_sem.at[0], e_sem.at[1], parts[0], -1)
    c_copies[1].wait_recv()
    for r in LEAVES:
        hop(1, r)
    send(se, re, e_sem.at[0], e_sem.at[1], parts[1], -1)
    for p in range(PIECES):
        for r in INNER_NEAR:
            hop(p, r)
    backward(1)
    for r in INNER_FAR:
        hop(0, r)
    backward(0)
    ri[0] = si[0]
    for r in INNER_FAR:
        hop(1, r)
    spread_w = place_w[...].reshape(whole, tokens).T
    high = spread_w.astype(BF16)
    low = (spread_w - high.astype(F32)).astype(BF16)
    spread_one = place[...].astype(F32).reshape(whole, tokens).T.astype(BF16)
    sent(sx, x_sem.at[0], x_sem.at[1])
    for p in range(PIECES):
        sent(sg.at[p], g_sem.at[0, p], g_sem.at[1, p])
        c_copies[p].wait_send()
    arrived(re, e_sem.at[0], e_sem.at[1], every)
    returned = re[...].reshape(whole, width)
    summed = jnp.dot(high, returned, preferred_element_type=F32)
    summed += jnp.dot(low, returned, preferred_element_type=F32)
    out_ref[...] = summed.astype(BF16)
    arrived(ri, i_sem.at[0], i_sem.at[1], every)
    grad_ref[...] = jnp.dot(
        spread_one, ri[...].reshape(whole, width), preferred_element_type=F32).astype(BF16)
    sent(se, e_sem.at[0], e_sem.at[1])
    sent(si, i_sem.at[0], i_sem.at[1])
    for p in range(PIECES):
        down_ref[:, p * piece:(p + 1) * piece] = partial(p, 0)
    bulk(hop_s, hop_s, hop_sent, hop_sem.at[0, 0]).wait_send()


def store(*refs):
    copies = [pltpu.make_async_copy(refs[i], refs[3 + i], refs[6].at[i]) for i in range(3)]
    for copy in copies:
        copy.start()
    for copy in copies:
        copy.wait()


def local(latents, routes, gate_level, cotangent, w_gate, w_up, w_down):
    tokens, width = latents.shape
    hidden = w_gate.shape[2]
    whole = SLOTS * CAP
    z_count = lax.axis_size("dp") // 2
    block = (SLOTS, CAP, width)
    piece = width // PIECES
    sums = (PIECES, z_count, 16, piece)
    hop_count = len(HOPS)
    anywhere = pl.BlockSpec(memory_space=pl.ANY)
    in_vmem = pl.BlockSpec(memory_space=pltpu.VMEM)
    dma = pltpu.SemaphoreType.DMA
    results = pl.pallas_call(
        kernel,
        out_shape=(
            pltpu.VMEM((tokens, width), BF16),
            pltpu.VMEM((tokens, width), BF16),
            pltpu.VMEM((16, width), F32),
        ),
        in_specs=[anywhere] * 7,
        out_specs=(in_vmem,) * 3,
        scratch_shapes=[
            pltpu.VMEM(latents.shape, BF16),
            pltpu.VMEM(routes.shape[::-1], jnp.int32),
            pltpu.VMEM(gate_level.shape[::-1], jnp.int32),
            pltpu.VMEM(cotangent.shape, BF16),
            pltpu.VMEM((width, hidden), BF16),
            pltpu.VMEM((width, hidden), BF16),
            pltpu.VMEM((hidden, width), BF16),
            pltpu.VMEM((SLOTS, tokens), F32),
            pltpu.VMEM((SLOTS, tokens), F32),
            pltpu.VMEM((SLOTS, CAP, tokens), BF16),
            pltpu.VMEM((SLOTS, CAP, tokens), F32),
        ] + [pltpu.VMEM(block, BF16)] * 2 + [pltpu.VMEM((PIECES, SLOTS, CAP, piece), BF16)] * 2 + [
            pltpu.VMEM(block, BF16)] * 4 + [
            pltpu.VMEM((ROWS, hidden), BF16),
            pltpu.VMEM((2, z_count, 16, whole), BF16),
            pltpu.VMEM((whole, hidden), F32),
            pltpu.VMEM((whole, hidden), F32),
            pltpu.VMEM(sums, F32),
            pltpu.VMEM(sums, BF16),
            pltpu.VMEM(sums, BF16),
            pltpu.VMEM((PIECES, hop_count, 16, piece), BF16),
            pltpu.VMEM((PIECES, hop_count, 16, piece), BF16),
            dma((7,)), dma((1 + GROUPS,)), dma((2, PIECES)), dma((2,)), dma((2,)),
            dma((2, PIECES)), dma((PIECES, len(CHILDREN))), dma, pltpu.SemaphoreType.REGULAR((2,)),
        ],
        compiler_params=pltpu.CompilerParams(
            collective_id=0, has_side_effects=True, vmem_limit_bytes=56 << 20),
        name="moe",
    )(latents, routes.T, gate_level.T, cotangent, w_gate[0], w_up[0], w_down[0])
    latent_out, grad_latents, grad_down = pl.pallas_call(
        store,
        out_shape=[jax.ShapeDtypeStruct(r.shape, r.dtype) for r in results],
        in_specs=[anywhere] * 3,
        out_specs=[anywhere] * 3,
        scratch_shapes=[dma((3,))],
        name="store",
    )(*[pltpu.with_memory_space_constraint(r, pltpu.VMEM) for r in results])
    return latent_out, grad_latents, grad_down[None]


def solution(mesh):
    return jax.shard_map(
        local,
        mesh=mesh,
        in_specs=(
            P(("dp", "expert"), None),
            P(("dp", "expert"), None),
            P(("dp", "expert"), None),
            P(("dp", "expert"), None),
            P("expert", None, None),
            P("expert", None, None),
            P("expert", None, None),
        ),
        out_specs=(P(("dp", "expert"), None), P(("dp", "expert"), None), P("expert", "dp", None)),
        check_vma=False,
    )
```
